256 devices in a mesh: tm: 4 (over y), rows: 32 (over x_lo, z, core), rep: 2 (over x_hi).
Axes of the slice: x: 4 (x_hi: 2, x_lo: 2; x = x_hi * 2 + x_lo), y: 4, z: 8, core: 2. Of those that a mesh axis runs over, the one named last changes fastest.
Arguments:
- latent: bfloat16 [4, 16, 16, 128, 128], P('rep', None, 'tm', 'rows'), may hold values from -6 to 6
- weight: bfloat16 [384, 432], replicated, may hold values from -0.3125 to 0.3125
- cotangent: bfloat16 [4, 384, 16, 128, 128], P('rep', None, 'tm', 'rows'), may hold values from -6 to 6
- frame_group_index: int32 [4, 16], P('rep'), may hold values from 0 to 2, never falling along the last dimension, each value on 1 to 8 neighbouring positions
- sequence_token_order: int32 [65536], replicated, may hold values from 0 to 65535, as said below
Outputs:
- sequence_token_gradient: bfloat16 [4, 32768, 128], P('rep', ('tm', 'rows'))
- weight_gradient: float32 [384, 432], replicated
The draws below stay inside these ranges and needn't reach their ends.
Inputs may be any that keep to these rules, and one draw needn't show every extreme that they name: `frame_group_index`: Frame-group numbers never fall along a clip's frames. A permutation of a clip's tokens. Call the tokens of frames t * 4 to t * 4 + 3 and half-rows r * (2) to r * 2 + 4 // 2 - 1 the block of (t, r), numbered t * 32 + r; every 512 positions in a row of sequence_token_order (positions j * 512 onward) hold exactly 4 tokens of every block.
All inputs are finite; a program needn't handle non-finite values.
Results may differ from the reference program's by a relative error of at most 0.0065.
Values may be sent and summed in bfloat16 or wider, within the bound.
No kernel may reach another device: no remote copies, remote signals or barrier semaphores. Data moves between devices by JAX's collectives and lax.ppermute only.
A program may use at most 128 MiB of HBM per device.

```python
import math
import jax
import jax.numpy as jnp
import numpy as np
from jax import lax

ZC = 16
CH = 384
TF = 4
RB = 4
W = 128
PATCH = 64
CLIPS = 4
FRAMES = 16
HEIGHT = 128
TOK_DEV = 512
TOKENS = 65536
N_TM = 4
N_ROWS = 32


def draw_sequence_token_order(key, part):
    key = jax.random.fold_in(key, 7)
    peers = N_TM * N_ROWS
    local_portion = TOK_DEV // peers
    half_rows = RB // 2
    half_cols = W // 2
    first_key, second_key = jax.random.split(key)
    local_order = jax.vmap(lambda subkey: jax.random.permutation(subkey, TOK_DEV))(jax.random.split(first_key, peers))
    sender_index = jnp.arange(peers, dtype=jnp.int32)[:, None]
    time_part = sender_index // N_ROWS
    band_part = sender_index % N_ROWS
    frame_loc = local_order // (half_rows * half_cols)
    row_loc = local_order // half_cols % half_rows
    col_loc = local_order % half_cols
    natural = ((time_part * TF + frame_loc) * (half_rows * N_ROWS) + band_part * half_rows + row_loc) * half_cols + col_loc
    blocks = natural.reshape(peers, peers, local_portion).transpose(1, 0, 2).reshape(peers, TOK_DEV)
    mixing = jax.vmap(lambda subkey: jax.random.permutation(subkey, TOK_DEV))(jax.random.split(second_key, peers))
    shuffled = jnp.take_along_axis(blocks, mixing, axis=1)
    return shuffled.reshape(-1).astype(jnp.int32)


def block_levels(own_key, shape, shards, least, top_value):
    def one(axis_at, blocks):
        draws = jax.random.uniform(jax.random.fold_in(jax.random.fold_in(own_key, 6), axis_at), (blocks,), jnp.float32, least / len(shards), top_value / len(shards))
        return jnp.repeat(jnp.exp(draws), shape[axis_at] // blocks).reshape((-1,) + (1,) * (len(shape) - axis_at - 1))

    level = one(*shards[0])
    for cut in shards[1:]:
        level = level * one(*cut)
    return level


def length_profile(number_of, total, bound, lean):
    weights = [(1 << 20) // math.isqrt(standing ** lean) + 1 for standing in range(2, number_of + 1)]
    spare, given = total - bound - (number_of - 1), [1] * (number_of - 1)
    while spare > 0:
        movable = [i for i in range(number_of - 1) if given[i] < bound]
        mass, remaining = sum([weights[i] for i in movable]), spare
        for i in movable:
            more = min(bound - given[i], max(1, remaining * weights[i] // mass), spare)
            given[i] = given[i] + more
            spare = spare - more
    return np.array([bound] + given)


def uneven(stream_key, amount, total, bound, slope):
    if amount == 2:
        one = jax.random.randint(stream_key, (), max(1, total - bound), min(bound, total - 1) + 1)
        return jnp.stack([one, total - one])
    sizes = jnp.asarray(length_profile(amount, total, bound, slope), jnp.int32)
    couples = (amount - 1) // 2
    giver, taker = sizes[1:1 + 2 * couples:2], sizes[2:2 + 2 * couples:2]
    room = jnp.minimum(giver - 1, bound - taker)
    shifted = jax.random.randint(jax.random.fold_in(stream_key, 1), (couples,), 0, 1 << 20) % (room + 1)
    sizes = sizes.at[1:1 + 2 * couples:2].set(giver - shifted).at[2:2 + 2 * couples:2].set(taker + shifted)
    return sizes[jax.random.permutation(jax.random.fold_in(stream_key, 2), amount)]


def centred(rng, shape, scale, reach, cuts=(), kind=jnp.bfloat16):
    result = jax.random.normal(rng, shape, jnp.float32) * scale
    if len(cuts) > 0:
        result = block_levels(rng, shape, cuts, -0.22, 0.18) * result
    return jnp.clip(result, min=-reach, max=reach).astype(kind)


def setup_inputs(seed: int = 0) -> dict:
    key_list = jax.random.split(jax.random.key(seed), 6)
    return {
        "latent": centred(key_list[0], (CLIPS, ZC, FRAMES, HEIGHT, W), 1.0, 6.0, ((0, 2), (2, 4), (3, 32))),
        "weight": centred(key_list[1], (CH, 27 * ZC), (27 * ZC) ** -0.5, 0.3125),
        "cotangent": centred(key_list[2], (CLIPS, CH, FRAMES, HEIGHT, W), 1.0, 6.0, ((0, 2), (2, 4), (3, 32))),
        "frame_group_index": jax.vmap(lambda own: jnp.searchsorted(jnp.cumsum(uneven(own, 3, FRAMES, FRAMES // 2, 2)), jnp.arange(FRAMES), side="right"))(jax.random.split(key_list[3], CLIPS)).reshape((CLIPS, FRAMES)).astype(jnp.int32),
        "sequence_token_order": draw_sequence_token_order(jax.random.fold_in(key_list[5], 71), 0),
    }


def frame_masks(segs):
    masks = []
    for t_off in range(3):
        back = 2 - t_off
        if back > 0:
            earlier = jnp.concatenate([jnp.full((back,), -1, jnp.int32), segs[:FRAMES - back]])
        else:
            earlier = segs
        masks.append((earlier == segs).astype(jnp.float32))
    return masks

def single_clip(input_arrays, weight, sequence_token_order):
    lat, cot, segs = input_arrays
    masks = frame_masks(segs)
    padded = jnp.pad(lat, ((0, 0), (2, 0), (1, 1), (1, 1)))
    pieces = []
    for t_off in range(3):
        factor = masks[t_off].astype(jnp.bfloat16)[None, :, None, None]
        for h_off in range(3):
            for w_off in range(3):
                pieces.append(padded[:, t_off:t_off + FRAMES, h_off:h_off + HEIGHT, w_off:w_off + W] * factor)
    patches = jnp.stack(pieces, 0).reshape(27 * ZC, FRAMES * HEIGHT * W)
    pre = jnp.dot(weight, patches, preferred_element_type=jnp.float32)
    sig = jax.nn.sigmoid(pre)
    grad_pre = (cot.reshape(CH, -1).astype(jnp.float32) * sig * (1.0 + pre * (1.0 - sig))).astype(jnp.bfloat16)
    grad_part = jnp.dot(grad_pre, patches.T, preferred_element_type=jnp.float32)
    contrib = jnp.dot(weight.T, grad_pre, preferred_element_type=jnp.float32).reshape(27, ZC, FRAMES, HEIGHT, W)
    spread = jnp.zeros((ZC, FRAMES + 2, HEIGHT + 2, W + 2), jnp.float32)
    for t_off in range(3):
        factor = masks[t_off][None, :, None, None]
        for h_off in range(3):
            for w_off in range(3):
                tap = t_off * 9 + h_off * 3 + w_off
                spread = spread.at[:, t_off:t_off + FRAMES, h_off:h_off + HEIGHT, w_off:w_off + W].add(contrib[tap] * factor)
    latent_grad = spread[:, 2:, 1:HEIGHT + 1, 1:W + 1].astype(jnp.bfloat16)
    tokens = latent_grad.reshape(ZC, FRAMES, HEIGHT // 2, 2, W // 2, 2)
    tokens = tokens.transpose(1, 2, 4, 0, 3, 5).reshape(TOKENS, PATCH)
    ordered = jnp.take(tokens, sequence_token_order, axis=0).reshape(TOKENS // 2, 2 * PATCH)
    return (ordered, grad_part)

def reference(latent, weight, cotangent, frame_group_index, sequence_token_order):
    sequence_token_gradient, gradient_portions = lax.map(lambda input_arrays: single_clip(input_arrays, weight, sequence_token_order), (latent, cotangent, frame_group_index))
    scale = 1.0 / math.sqrt(CLIPS * FRAMES * HEIGHT * W)
    weight_gradient = lax.optimization_barrier(jnp.sum(gradient_portions, axis=0)) * scale
    return (sequence_token_gradient, weight_gradient)
```

```python
import math

import jax
import jax.numpy as jnp
from jax import lax
from jax.experimental import pallas as pl
from jax.experimental.pallas import tpu as pltpu
from jax.sharding import Mesh, PartitionSpec as P

BF = jnp.bfloat16
F32 = jnp.float32
BAND = ("xl", "z", "core")
PEERS = ("tm", "xl", "z", "core")
NT = (((1,), (1,)), ((), ()))
VMEM = 48 * 1024 * 1024


def matmul(a, b):
    return jnp.dot(a, b, preferred_element_type=F32)


def matmul_nt(a, b):
    return lax.dot_general(a, b, NT, preferred_element_type=F32)


def call(body, outs, cost, scratch=(), grid=None, in_specs=None, out_specs=None):
    params = {}
    if grid is not None:
        params = {"grid": grid, "in_specs": in_specs, "out_specs": out_specs}
    elif in_specs is not None:
        params = {"in_specs": in_specs}
    return pl.pallas_call(
        body,
        out_shape=outs,
        scratch_shapes=list(scratch),
        cost_estimate=pl.CostEstimate(flops=int(cost[0]), bytes_accessed=int(cost[1]), transcendentals=0),
        compiler_params=pltpu.CompilerParams(vmem_limit_bytes=VMEM),
        **params,
    )


def ones_where(cond):
    return jnp.where(cond, 1.0, 0.0).astype(BF)


def select_body(me_ref, order_ref, own_ref, pair_ref, send_ref, take_ref):
    me = me_ref[0]
    order = order_ref[...]
    frame = order >> 12
    row = (order >> 6) & 63
    mine = ((frame >> 2) * 32 + (row >> 1)) == me
    local_id = ((frame & 3) * 2 + (row & 1)) * 64 + (order & 63)
    up = lax.broadcasted_iota(jnp.int32, (512, 512), 0)
    lane = lax.broadcasted_iota(jnp.int32, (512, 512), 1)
    running = matmul(ones_where(mine), ones_where(up <= lane))
    spread = ones_where(
        (lax.broadcasted_iota(jnp.int32, (512, 128), 0) >> 2)
        == lax.broadcasted_iota(jnp.int32, (512, 128), 1)
    )
    slot = lax.broadcasted_iota(jnp.int32, (512, 1), 0) & 3
    source = jnp.zeros((512, 1), F32)
    for s in range(4):
        hit = mine & (running == s + 1.0)
        value = jnp.sum(jnp.where(hit, local_id, 0).astype(F32), axis=1, keepdims=True)
        high = jnp.floor(value * (1.0 / 16.0))
        low = value - high * 16.0
        high = matmul(spread, jnp.broadcast_to(high, (128, 128)).astype(BF))
        low = matmul(spread, jnp.broadcast_to(low, (128, 128)).astype(BF))
        source = source + jnp.where(slot == s, (high * 16.0 + low)[:, 0:1], 0.0)
    place = 2 * source.astype(jnp.int32)
    send_ref[...] = ones_where(lax.broadcasted_iota(jnp.int32, (512, 1024), 1) == place)
    own = own_ref[...]
    sender = (own >> 14) * 32 + ((own >> 7) & 31)
    pairs = pair_ref[...]
    pos = lax.broadcasted_iota(jnp.int32, (256, 512), 1)
    half = lax.broadcasted_iota(jnp.int32, (256, 512), 0)
    for e in range(2):
        mate = pairs[:, e : e + 1]
        mate = (mate >> 14) * 32 + ((mate >> 7) & 31)
        earlier = (sender == mate) & (pos < 2 * half + e)
        count = jnp.sum(jnp.where(earlier, 1.0, 0.0), axis=1, keepdims=True)
        take_ref[e] = ones_where(pos == mate * 4 + count.astype(jnp.int32))


def main_body(
    tm_ref, seg_ref, prev_ref, lat_ref, low_ref, high_ref, cot_ref, w_ref, wt_ref,
    wg_ref, own_ref, glow_ref, ghigh_ref, gprev_ref,
    ext, patch, total, spread,
):
    b = pl.program_id(0)
    f = pl.program_id(1)
    lanes = lax.broadcasted_iota(jnp.int32, (1, 128), 1)

    @pl.when((b == 0) & (f == 0))
    def _():
        patch[432:512, :] = jnp.zeros((80, 512), BF)
        total[...] = jnp.zeros_like(total)

    @pl.when(f == 0)
    def _():
        spread[...] = jnp.zeros_like(spread)
        ext[1, 0:2, 1:5] = prev_ref[0]
        ext[1, 2:6, 1:5] = lat_ref[0]
        ext[1, :, 0] = low_ref[0]
        ext[1, :, 5] = high_ref[0]
        for fr in range(6):
            x = ext[1, fr].astype(F32).reshape(96, 128)
            left = jnp.where(lanes == 0, 0.0, pltpu.roll(x, 1, 1))
            right = jnp.where(lanes == 127, 0.0, pltpu.roll(x, 127, 1))
            ext[0, fr] = left.astype(BF).reshape(6, 16, 128)
            ext[2, fr] = right.astype(BF).reshape(6, 16, 128)

    frame = tm_ref[0] * 4 + f
    seg = seg_ref[b, frame]
    factors = []
    for a in range(3):
        before = frame - (2 - a)
        same = (before >= 0) & (seg_ref[b, jnp.maximum(before, 0)] == seg)
        factors.append(jnp.where(same, 1.0, 0.0))
    for a in range(3):
        mask = jnp.full((16, 128), factors[a], F32).astype(BF)
        for r in range(3):
            for c in range(3):
                top = (a * 9 + r * 3 + c) * 16
                for h in range(4):
                    patch[top : top + 16, h * 128 : h * 128 + 128] = ext[c, f + a, h + r] * mask
    patches = patch[...]
    pre = matmul(w_ref[...], patches)
    sig = 0.5 * jnp.tanh(0.5 * pre) + 0.5
    grad = (cot_ref[0].astype(F32) * sig * (1.0 + pre * (1.0 - sig))).astype(BF)
    total[...] += matmul_nt(grad, patches)
    back = matmul(wt_ref[...], grad)
    for a in range(3):
        for c in range(3):
            for row in range(6):
                acc = None
                for r in range(3):
                    h = row - r
                    if 0 <= h < 4:
                        top = (a * 9 + r * 3 + c) * 16
                        term = back[top : top + 16, h * 128 : h * 128 + 128]
                        acc = term if acc is None else acc + term
                spread[c, f + a, row] += acc * factors[a]

    @pl.when(f == 3)
    def _():
        for fr in range(6):
            x0 = spread[0, fr].reshape(96, 128)
            x2 = spread[2, fr].reshape(96, 128)
            x = (
                spread[1, fr].reshape(96, 128)
                + jnp.where(lanes == 127, 0.0, pltpu.roll(x0, 127, 1))
                + jnp.where(lanes == 0, 0.0, pltpu.roll(x2, 1, 1))
            ).reshape(6, 16, 128)
            glow_ref[0, fr] = x[0].astype(BF)
            ghigh_ref[0, fr] = x[5].astype(BF)
            if fr < 2:
                gprev_ref[0, fr] = x[1:5]
            else:
                own_ref[0, fr - 2] = x[1:5]

    @pl.when((b == 1) & (f == 3))
    def _():
        wg_ref[...] = total[...].astype(wg_ref.dtype)


def out_body(own_ref, low_ref, high_ref, next_ref, send_ref, out_ref, rows):
    for b in range(2):
        for f in range(4):
            for h in range(4):
                x = own_ref[b, f, h]
                if h == 0:
                    x = x + low_ref[b, 2 + f].astype(F32)
                if h == 3:
                    x = x + high_ref[b, 2 + f].astype(F32)
                if f >= 2:
                    x = x + next_ref[b, f - 2, h].astype(F32)
                x = x.astype(BF)
                top = (b * 2 + h % 2) * 16
                col = (f * 2 + h // 2) * 128
                rows[top : top + 16, col : col + 128] = x
                rows[64 + top : 80 + top, col : col + 128] = pltpu.roll(x.astype(F32), 127, 1).astype(BF)
    out_ref[...] = matmul_nt(send_ref[...], rows[...]).astype(BF)


def take_body(got_ref, take_ref, out_ref):
    src = lax.broadcasted_iota(jnp.int32, (128, 128), 0)
    dst = lax.broadcasted_iota(jnp.int32, (128, 128), 1)
    want = ((dst & 1) << 6) + (((dst >> 1) & 1) << 4) + ((dst >> 2) & 15)
    got = got_ref[...]
    for b in range(2):
        total = None
        for e in range(2):
            place = ones_where((src == want + b * 32) & ((dst >> 6) == e))
            moved = matmul(got, place).astype(BF)
            term = matmul(take_ref[e], moved)
            total = term if total is None else total + term
        out_ref[b] = total.astype(BF)


def reduce_weight(wg):
    every = ("rep",) + PEERS
    parts = exchange(wg.reshape(256, 6, 128), every)
    part = jnp.sum(parts.astype(F32), axis=0).astype(BF)
    whole_sum = exchange(jnp.broadcast_to(part[None], (256, 6, 128)), every)
    cells = math.sqrt(4 * 16 * 128 * 128)
    return whole_sum.reshape(384, 512)[:, :432].astype(F32) * (1.0 / cells)


def shifted(value, axes, step):
    count = math.prod(lax.axis_size(a) for a in axes)
    pairs = [(i, i + step) for i in range(count) if 0 <= i + step < count]
    return lax.ppermute(value, axes, pairs)


def exchange(value, axes):
    return lax.all_to_all(value, axes, split_axis=0, concat_axis=0, tiled=True)


def whole(shape):
    return pl.BlockSpec(shape, lambda b, f: (0,) * len(shape))


def on_device(latent, weight, cotangent, groups, order):
    tm = lax.axis_index("tm")
    band = lax.axis_index(BAND)
    me = tm * 32 + band
    smem = pl.BlockSpec(memory_space=pltpu.SMEM)
    vmem = pl.BlockSpec(memory_space=pltpu.VMEM)
    lat = latent.transpose(0, 2, 3, 1, 4)
    prev = shifted(lat[:, 2:4], ("tm",), 1)
    low = shifted(jnp.concatenate([prev[:, :, 3], lat[:, :, 3]], axis=1), BAND, 1)
    high = shifted(jnp.concatenate([prev[:, :, 0], lat[:, :, 0]], axis=1), BAND, -1)
    rows = order.reshape(128, 512)
    own = lax.dynamic_slice_in_dim(rows, me, 1, axis=0)
    send, take = call(
        select_body,
        (jax.ShapeDtypeStruct((512, 1024), BF), jax.ShapeDtypeStruct((2, 256, 512), BF)),
        (500e6, 2e6),
        in_specs=[smem, vmem, vmem, vmem],
    )(me.reshape(1), rows, own, own.reshape(256, 2))
    cot = cotangent.reshape(2, 384, 2048)
    padded = jnp.pad(weight, ((0, 0), (0, 80)))
    per_clip = lambda *shape: pl.BlockSpec((1,) + shape, lambda b, f: (b,) + (0,) * len(shape))
    wg, grad, glow, ghigh, gprev = call(
        main_body,
        (
            jax.ShapeDtypeStruct((384, 512), BF),
            jax.ShapeDtypeStruct((2, 4, 4, 16, 128), F32),
            jax.ShapeDtypeStruct((2, 6, 16, 128), BF),
            jax.ShapeDtypeStruct((2, 6, 16, 128), BF),
            jax.ShapeDtypeStruct((2, 2, 4, 16, 128), F32),
        ),
        (4.5e9, 5e6),
        scratch=[
            pltpu.VMEM((3, 6, 6, 16, 128), BF),
            pltpu.VMEM((512, 512), BF),
            pltpu.VMEM((384, 512), F32),
            pltpu.VMEM((3, 6, 6, 16, 128), F32),
        ],
        grid=(2, 4),
        in_specs=[
            smem,
            smem,
            per_clip(2, 4, 16, 128),
            per_clip(4, 4, 16, 128),
            per_clip(6, 16, 128),
            per_clip(6, 16, 128),
            pl.BlockSpec((1, 384, 512), lambda b, f: (b, 0, f)),
            whole((384, 512)),
            whole((432, 384)),
        ],
        out_specs=[
            whole((384, 512)),
            per_clip(4, 4, 16, 128),
            per_clip(6, 16, 128),
            per_clip(6, 16, 128),
            per_clip(2, 4, 16, 128),
        ],
    )(tm.reshape(1), groups, prev, lat, low, high, cot, padded, weight.T)
    weight_gradient = reduce_weight(wg)
    from_low = shifted(ghigh, BAND, 1)
    from_high = shifted(glow, BAND, -1)
    early = gprev.at[:, :, 0].add(from_low[:, 0:2].astype(F32))
    early = early.at[:, :, 3].add(from_high[:, 0:2].astype(F32)).astype(BF)
    from_next = shifted(early, ("tm",), -1)
    outgoing = call(
        out_body,
        jax.ShapeDtypeStruct((512, 128), BF),
        (150e6, 2e6),
        scratch=[pltpu.VMEM((128, 1024), BF)],
        in_specs=[vmem] * 5,
    )(grad, from_low, from_high, from_next, send)
    got = exchange(outgoing.reshape(128, 4, 128), PEERS).reshape(512, 128)
    tokens = call(
        take_body,
        jax.ShapeDtypeStruct((2, 256, 128), BF),
        (200e6, 1e6),
        in_specs=[vmem] * 2,
    )(got, take)
    return tokens, weight_gradient


def solution(mesh):
    split = Mesh(mesh.devices.reshape(4, 2, 8, 2, 2), ("tm", "xl", "z", "core", "rep"))
    placed = P("rep", None, "tm", BAND, None)
    return jax.shard_map(
        on_device,
        mesh=split,
        in_specs=(placed, P(), placed, P("rep", None), P()),
        out_specs=(P("rep", PEERS, None), P()),
        check_vma=False,
    )
```

```python
import math

import jax
import jax.numpy as jnp
from jax import lax
from jax.experimental import pallas as pl
from jax.experimental.pallas import tpu as pltpu
from jax.sharding import Mesh, PartitionSpec as P

BF = jnp.bfloat16
F32 = jnp.float32
BAND = ("xl", "z", "core")
PEERS = ("tm", "xl", "z", "core")
CHIPS = ("xl", "z", "tm")
NT = (((1,), (1,)), ((), ()))


def matmul(a, b):
    return jnp.dot(a, b, preferred_element_type=F32)


def matmul_nt(a, b):
    return lax.dot_general(a, b, NT, preferred_element_type=F32)


def call(body, outs, cost, scratch=(), grid=None, in_specs=None, out_specs=None, vmem=16):
    params = {}
    if grid is not None:
        params = {"grid": grid, "in_specs": in_specs, "out_specs": out_specs}
    elif in_specs is not None:
        params = {"in_specs": in_specs}
    return pl.pallas_call(
        body,
        out_shape=outs,
        scratch_shapes=list(scratch),
        cost_estimate=pl.CostEstimate(flops=int(cost[0]), bytes_accessed=int(cost[1]), transcendentals=0),
        compiler_params=pltpu.CompilerParams(vmem_limit_bytes=vmem * 1024 * 1024),
        **params,
    )


def ones_where(cond):
    return jnp.where(cond, 1.0, 0.0).astype(BF)


def select_body(me_ref, order_hbm, wt_hbm, send_ref, take_ref, wide_ref, order_ref, wt_ref, tall, sems):
    copies = [pltpu.make_async_copy(order_hbm, order_ref, sems.at[0]), pltpu.make_async_copy(wt_hbm, wt_ref, sems.at[1])]
    copies[0].start()
    copies[1].start()
    copies[0].wait()
    me = me_ref[0]
    order = order_ref[...]
    mine = ((order >> 14) * 32 + ((order >> 7) & 31)) == me
    local_id = (((order >> 12) & 3) * 2 + ((order >> 6) & 1)) * 64 + (order & 63)
    hits = ones_where(mine)
    up = lax.broadcasted_iota(jnp.int32, (128, 128), 0)
    lane = lax.broadcasted_iota(jnp.int32, (128, 128), 1)
    running = matmul(hits, ones_where(up <= lane))
    row = lax.broadcasted_iota(jnp.int32, (512, 512), 0)
    col = lax.broadcasted_iota(jnp.int32, (512, 512), 1)
    group = (row >> 2) == (col >> 2)
    above = matmul(ones_where(group & (col < row)), hits)
    running = running + jnp.sum(above, axis=1, keepdims=True)
    lane = lax.broadcasted_iota(jnp.int32, (512, 128), 1)
    slot = lax.broadcasted_iota(jnp.int32, (512, 128), 0) & 3
    found = jnp.zeros((512, 128), F32)
    for s in range(4):
        hit = mine & (running == s + 1.0)
        high = jnp.sum(jnp.where(hit, local_id >> 4, 0).astype(F32), axis=1, keepdims=True)
        low = jnp.sum(jnp.where(hit, local_id & 15, 0).astype(F32), axis=1, keepdims=True)
        found = found + jnp.where(lane == s, high, 0.0) + jnp.where(lane == s + 4, low, 0.0)
    found = matmul(ones_where(group), found.astype(BF))
    found = jnp.where(lane == slot, found * 16.0, 0.0) + jnp.where(lane == slot + 4, found, 0.0)
    place = 2 * jnp.sum(found, axis=1, keepdims=True).astype(jnp.int32)
    send_ref[...] = jnp.broadcast_to(place, (512, 128))
    pair = order_ref[pl.ds(pl.multiple_of((me >> 1) * 8, 8), 8), :]
    four = jnp.where((me & 1) == 0, pair[0:4], pair[4:8])
    own = jnp.concatenate([four[i : i + 1] for i in range(4)], axis=1)
    sender = (own >> 14) * 32 + ((own >> 7) & 31)
    pos = lax.broadcasted_iota(jnp.int32, (256, 512), 1)
    half = lax.broadcasted_iota(jnp.int32, (256, 512), 0)
    for e in range(2):
        here = pos == 2 * half + e
        mate = jnp.sum(jnp.where(here, sender, 0).astype(F32), axis=1, keepdims=True).astype(jnp.int32)
        earlier = (sender == mate) & (pos < 2 * half + e)
        count = jnp.sum(jnp.where(earlier, 1.0, 0.0), axis=1, keepdims=True)
        far = jnp.where((mate & 1) == (me & 1), 0, 256)
        take_ref[e] = jnp.broadcast_to(far + (mate >> 1) * 4 + count.astype(jnp.int32), (256, 128))
    copies[1].wait()
    tall[0:432, :] = wt_ref[...].astype(F32)
    tall[432:512, :] = jnp.zeros((80, 384), F32)
    wide_ref[...] = tall[...].T.astype(BF)


def main_body(
    tm_ref, core_ref, seg_ref, prev_hbm, lat_hbm, near_hbm, far_hbm, cot_hbm, wide_hbm, wt_hbm,
    keep_hbm, pair_hbm, own_hbm, gfar_hbm, gprev_hbm,
    prev, lat, near, far, cot, wide, wt, ext, patch0, patch1, pre0, pre1, total, spread,
    keep, pair, own, gfar, gprev, edges, sems, cot_sems, out_sems,
):
    lanes = lax.broadcasted_iota(jnp.int32, (1, 128), 1)
    near_row = 5 - 5 * core_ref[0]
    ins = [(prev_hbm, prev), (lat_hbm, lat), (near_hbm, near), (far_hbm, far), (wide_hbm, wide), (wt_hbm, wt)]
    ins = [pltpu.make_async_copy(src, dst, sems.at[i]) for i, (src, dst) in enumerate(ins)]
    for copy in ins:
        copy.start()

    def cot_copy(i):
        return pltpu.make_async_copy(cot_hbm.at[i >> 2, :, i & 3], cot.at[i], cot_sems.at[i])

    for i in range(8):
        cot_copy(i).start()
    patch0[432:512, :] = jnp.zeros((80, 512), BF)
    patch1[432:512, :] = jnp.zeros((80, 512), BF)
    total[...] = jnp.zeros_like(total)
    spread[...] = jnp.zeros_like(spread)
    for copy in ins[:4]:
        copy.wait()
    for b in range(2):
        for h in range(4):
            ext[b, 1, 0:2, 1 + h] = prev[h, b]
            ext[b, 1, 2:6, 1 + h] = lat[h, b]
        ext[b, 1, :, near_row] = near[b]
        ext[b, 1, :, 5 - near_row] = far[b]
        for fr in range(6):
            x = ext[b, 1, fr].astype(F32).reshape(96, 128)
            left = jnp.where(lanes == 0, 0.0, pltpu.roll(x, 1, 1))
            right = jnp.where(lanes == 127, 0.0, pltpu.roll(x, 127, 1))
            ext[b, 0, fr] = left.astype(BF).reshape(6, 16, 128)
            ext[b, 2, fr] = right.astype(BF).reshape(6, 16, 128)

    def factors(i):
        b = i >> 2
        frame = tm_ref[0] * 4 + (i & 3)
        seg = seg_ref[b, frame]
        result = []
        for a in range(3):
            before = frame - (2 - a)
            same = (before >= 0) & (seg_ref[b, jnp.maximum(before, 0)] == seg)
            result.append(jnp.where(same, 1.0, 0.0))
        return result

    def forward(i, patch, pre):
        b, f = i >> 2, i & 3
        masks = factors(i)
        for a in range(3):
            mask = jnp.full((16, 128), masks[a], F32).astype(BF)
            for r in range(3):
                for c in range(3):
                    top = (a * 9 + r * 3 + c) * 16
                    for h in range(4):
                        patch[top : top + 16, h * 128 : h * 128 + 128] = ext[b, c, f + a, h + r] * mask
        pre[...] = matmul(wide[...], patch[...])

    def backward(i, patch, pre):
        b, f = i >> 2, i & 3
        masks = factors(i)
        cot_copy(i).wait()
        cots = jnp.swapaxes(cot[i].astype(F32), 0, 1)
        grads = []
        for h in range(4):
            x = pre[:, h * 128 : h * 128 + 128]
            sig = 0.5 * jnp.tanh(0.5 * x) + 0.5
            grads.append((cots[h] * sig * (1.0 + x * (1.0 - sig))).astype(BF))
        grad = jnp.concatenate(grads, axis=1)
        total[...] += matmul_nt(patch[...], grad)
        back = matmul(wt[...], grad)
        for a in range(3):
            for c in range(3):
                for row in range(6):
                    acc = None
                    for r in range(3):
                        h = row - r
                        if 0 <= h < 4:
                            top = (a * 9 + r * 3 + c) * 16
                            term = back[top : top + 16, h * 128 : h * 128 + 128]
                            acc = term if acc is None else acc + term
                    spread[b, c, f + a, row] += acc * masks[a]

    for copy in ins[4:]:
        copy.wait()
    forward(0, patch0, pre0)

    def step(j, carry):
        i = 2 * j
        forward(i + 1, patch1, pre1)
        backward(i, patch0, pre0)
        forward(jnp.minimum(i + 2, 7), patch0, pre0)
        backward(i + 1, patch1, pre1)
        return carry

    lax.fori_loop(0, 4, step, 0)
    mine = core_ref[0] * 256
    for g in range(16):
        for i in range(3):
            cols = slice(i * 128, i * 128 + 128)
            kept = pl.multiple_of(mine + g * 16, 16)
            pair[g * 3 + i] = total[pl.ds(pl.multiple_of(256 - mine + g * 16, 16), 16), cols].astype(BF)
            keep[g * 3 + i] = total[pl.ds(kept, 16), cols].astype(BF)
    outs = [(pair, pair_hbm), (keep, keep_hbm), (gfar, gfar_hbm), (gprev, gprev_hbm), (own, own_hbm)]
    outs = [pltpu.make_async_copy(src, dst, out_sems.at[i]) for i, (src, dst) in enumerate(outs)]
    outs[1].start()
    for b in range(2):
        for fr in range(6):
            x0 = spread[b, 0, fr].reshape(96, 128)
            x2 = spread[b, 2, fr].reshape(96, 128)
            x = (
                spread[b, 1, fr].reshape(96, 128)
                + jnp.where(lanes == 127, 0.0, pltpu.roll(x0, 127, 1))
                + jnp.where(lanes == 0, 0.0, pltpu.roll(x2, 1, 1))
            ).reshape(6, 16, 128)
            edges[0] = x[0]
            edges[5] = x[5]
            pair[48 + b * 6 + fr] = edges[near_row].astype(BF)
            gfar[b, fr] = edges[5 - near_row].astype(BF)
            if fr < 2:
                gprev[b, fr] = x[1:5]
            else:
                own[b, fr - 2] = x[1:5]
    outs[0].start()
    for copy in outs[2:]:
        copy.start()
    for copy in outs:
        copy.wait()


def add_body(keep_ref, given_ref, out_ref):
    for g in range(16):
        for i in range(3):
            x = keep_ref[g * 3 + i].astype(F32) + given_ref[g * 3 + i].astype(F32)
            out_ref[g * 4 : g * 4 + 4, :, i * 128 : i * 128 + 128] = x.reshape(4, 4, 128).astype(BF)


def early_body(core_ref, gprev_ref, given_ref, far_ref, out_ref):
    near_row = 3 - 3 * core_ref[0]
    out_ref[...] = gprev_ref[...].astype(BF)
    for b in range(2):
        for f in range(2):
            near = given_ref[48 + b * 6 + f].astype(F32)
            out_ref[b, f, near_row] = (gprev_ref[b, f, near_row] + near).astype(BF)
            far = far_ref[b, f].astype(F32)
            out_ref[b, f, 3 - near_row] = (gprev_ref[b, f, 3 - near_row] + far).astype(BF)


def out_body(core_ref, own_ref, given_ref, far_ref, next_ref, send_ref, part_ref, twin_ref, out_ref, rows, grad):
    near_row = 3 - 3 * core_ref[0]
    grad[...] = own_ref[...]
    for b in range(2):
        for f in range(4):
            grad[b, f, near_row] += given_ref[50 + b * 6 + f].astype(F32)
            grad[b, f, 3 - near_row] += far_ref[b, 2 + f].astype(F32)
            for h in range(4):
                x = grad[b, f, h]
                if f >= 2:
                    x = x + next_ref[b, f - 2, h].astype(F32)
                x = x.astype(BF)
                top = (b * 2 + h % 2) * 16
                col = (f * 2 + h // 2) * 128
                rows[top : top + 16, col : col + 128] = x
                rows[64 + top : 80 + top, col : col + 128] = pltpu.roll(x.astype(F32), 127, 1).astype(BF)
    place = send_ref[...]
    lane = lax.broadcasted_iota(jnp.int32, (512, 128), 1)
    send = jnp.concatenate([ones_where(place == lane + i * 128) for i in range(8)], axis=1)
    tokens = matmul_nt(send, rows[...]).reshape(64, 2, 4, 128)
    out_ref[:, 0:2] = tokens.astype(BF)
    part = (part_ref[...] + twin_ref[...]) * (1.0 / math.sqrt(4 * 16 * 128 * 128))
    for i in range(3):
        piece = part[:, i * 128 : i * 128 + 128].astype(BF)
        out_ref[:, 2 + i] = jnp.broadcast_to(piece[None], (64, 4, 128))


def take_body(core_ref, mine_ref, other_ref, take_ref, out_ref, wg_ref):
    core = core_ref[0]
    got = jnp.concatenate([ref[:, core].astype(F32).reshape(256, 128) for ref in (mine_ref, other_ref)]).astype(BF)
    src = lax.broadcasted_iota(jnp.int32, (128, 128), 0)
    dst = lax.broadcasted_iota(jnp.int32, (128, 128), 1)
    lane = lax.broadcasted_iota(jnp.int32, (256, 128), 1)
    want = ((dst & 1) << 6) + (((dst >> 1) & 1) << 4) + ((dst >> 2) & 15)
    takes = []
    for e in range(2):
        row = take_ref[e]
        takes.append(jnp.concatenate([ones_where(row == lane + i * 128) for i in range(4)], axis=1))
    for b in range(2):
        total = None
        for e in range(2):
            place = ones_where((src == want + b * 32) & ((dst >> 6) == e))
            moved = matmul(got, place).astype(BF)
            term = matmul(takes[e], moved)
            total = term if total is None else total + term
        out_ref[b] = total.astype(BF)
    for i in range(3):
        mine = mine_ref[:, 2 + i].astype(F32)
        other = other_ref[:, 2 + i].astype(F32)
        halves = (jnp.where(core == 0, mine, other), jnp.where(core == 0, other, mine))
        for c in range(2):
            for j in range(64):
                top = c * 256 + (j & 15) * 16 + (j >> 4) * 4
                if top < 432:
                    wg_ref[top : top + 4, i * 128 : i * 128 + 128] = halves[c][j]


def shifted(value, step):
    count = lax.axis_size("tm")
    return lax.ppermute(value, "tm", [(i, i + step) for i in range(count) if 0 <= i + step < count])


def crossed(value):
    count = math.prod(lax.axis_size(a) for a in BAND)
    pairs = [(i, i + 1) for i in range(1, count - 1, 2)]
    return lax.ppermute(value, BAND, pairs + [(j, i) for i, j in pairs])


def swapped(value):
    return lax.ppermute(value, "core", [(0, 1), (1, 0)])


def exchange(value, axes):
    return lax.all_to_all(value, axes, split_axis=0, concat_axis=0, tiled=True)


def whole(shape):
    return pl.BlockSpec(shape, lambda b, f: (0,) * len(shape))


def on_device(latent, weight, cotangent, groups, order):
    tm = lax.axis_index("tm")
    core = lax.axis_index("core")
    me = tm * 32 + lax.axis_index(BAND)
    smem = pl.BlockSpec(memory_space=pltpu.SMEM)
    vmem = pl.BlockSpec(memory_space=pltpu.VMEM)
    hbm = pl.BlockSpec(memory_space=pltpu.HBM)
    tall = weight.T
    lat = latent.transpose(3, 0, 2, 1, 4)
    prev = shifted(lat[:, :, 2:4], 1)
    send, take, wide = call(
        select_body,
        (
            jax.ShapeDtypeStruct((512, 128), jnp.int32),
            jax.ShapeDtypeStruct((2, 256, 128), jnp.int32),
            jax.ShapeDtypeStruct((384, 512), BF),
        ),
        (500e6, 2e6),
        scratch=[
            pltpu.VMEM((512, 128), jnp.int32),
            pltpu.VMEM((432, 384), BF),
            pltpu.VMEM((512, 384), F32),
            pltpu.SemaphoreType.DMA((2,)),
        ],
        in_specs=[smem, hbm, hbm],
        vmem=60,
    )(me.reshape(1), order.reshape(512, 128), tall)
    prev, wide = lax.optimization_barrier((prev, wide))
    edge = lambda row: jnp.concatenate([lax.dynamic_index_in_dim(x, row, 0, False) for x in (prev, lat)], axis=1)
    far = crossed(edge(3 * core))
    near = swapped(edge(3 - 3 * core))
    outs = [
        ((48, 16, 128), BF),
        ((60, 16, 128), BF),
        ((2, 4, 4, 16, 128), F32),
        ((2, 6, 16, 128), BF),
        ((2, 2, 4, 16, 128), F32),
    ]
    keep, pair, grad, gfar, gprev = call(
        main_body,
        tuple(jax.ShapeDtypeStruct(*out) for out in outs),
        (4.5e9, 5e6),
        scratch=[
            pltpu.VMEM((4, 2, 2, 16, 128), BF),
            pltpu.VMEM((4, 2, 4, 16, 128), BF),
            pltpu.VMEM((2, 6, 16, 128), BF),
            pltpu.VMEM((2, 6, 16, 128), BF),
            pltpu.VMEM((8, 384, 4, 128), BF),
            pltpu.VMEM((384, 512), BF),
            pltpu.VMEM((432, 384), BF),
            pltpu.VMEM((2, 3, 6, 6, 16, 128), BF),
            pltpu.VMEM((512, 512), BF),
            pltpu.VMEM((512, 512), BF),
            pltpu.VMEM((384, 512), F32),
            pltpu.VMEM((384, 512), F32),
            pltpu.VMEM((512, 384), F32),
            pltpu.VMEM((2, 3, 6, 6, 16, 128), F32),
        ]
        + [pltpu.VMEM(*out) for out in outs]
        + [pltpu.VMEM((6, 16, 128), F32)]
        + [pltpu.SemaphoreType.DMA((n,)) for n in (6, 8, 5)],
        in_specs=[smem] * 3 + [hbm] * 7,
        out_specs=[hbm] * 5,
        vmem=60,
    )(tm.reshape(1), core.reshape(1), groups, prev, lat, near, far, cotangent, wide, tall)
    given = swapped(pair)
    half = call(add_body, jax.ShapeDtypeStruct((64, 4, 384), BF), (1e5, 6e5), in_specs=[vmem] * 2)(keep, given)
    from_far = crossed(gfar)
    early = call(
        early_body,
        jax.ShapeDtypeStruct((2, 2, 4, 16, 128), BF),
        (1e5, 3e5),
        in_specs=[smem] + [vmem] * 3,
    )(core.reshape(1), gprev, given, from_far)
    from_next = shifted(early, -1)
    parts = exchange(half, CHIPS)
    part = jnp.sum(parts.astype(F32), axis=0)
    twin = lax.ppermute(part, "rep", [(0, 1), (1, 0)])
    outgoing = call(
        out_body,
        jax.ShapeDtypeStruct((64, 5, 4, 128), BF),
        (150e6, 2e6),
        scratch=[pltpu.VMEM((128, 1024), BF), pltpu.VMEM((2, 4, 4, 16, 128), F32)],
        in_specs=[smem] + [vmem] * 7,
    )(core.reshape(1), grad, given, from_far, from_next, send, part, twin)
    got = exchange(outgoing, ("tm", "xl", "z"))
    other = swapped(got)
    tokens, summed = call(
        take_body,
        (jax.ShapeDtypeStruct((2, 256, 128), BF), jax.ShapeDtypeStruct((432, 384), F32)),
        (200e6, 1e6),
        in_specs=[smem] + [vmem] * 3,
    )(core.reshape(1), got, other, take)
    return tokens, summed.T


def solution(mesh):
    split = Mesh(mesh.devices.reshape(4, 2, 8, 2, 2), ("tm", "xl", "z", "core", "rep"))
    placed = P("rep", None, "tm", BAND, None)
    return jax.shard_map(
        on_device,
        mesh=split,
        in_specs=(placed, P(), placed, P("rep", None), P()),
        out_specs=(P("rep", PEERS, None), P()),
        check_vma=False,
    )
```

```python
import math

import jax
import jax.numpy as jnp
from jax import lax
from jax.experimental import pallas as pl
from jax.experimental.pallas import tpu as pltpu
from jax.sharding import Mesh, PartitionSpec as P

BF = jnp.bfloat16
F32 = jnp.float32
BAND = ("xl", "z", "core")
PEERS = ("tm", "xl", "z", "core")
CHIPS = ("xl", "z", "tm")
NT = (((1,), (1,)), ((), ()))


def matmul(a, b):
    return jnp.dot(a, b, preferred_element_type=F32)


def matmul_nt(a, b):
    return lax.dot_general(a, b, NT, preferred_element_type=F32)


MAIN_OUTS = [
    ((48, 16, 128), BF),
    ((60, 16, 128), BF),
    ((2, 4, 4, 16, 128), F32),
    ((2, 6, 16, 128), BF),
    ((2, 2, 4, 16, 128), F32),
]
MAIN_SCRATCH = [
    ((8, 384, 4, 128), BF),
    ((2, 3, 6, 6, 16, 128), BF),
    ((512, 512), BF),
    ((384, 512), F32),
    ((384, 512), F32),
    ((2, 3, 6, 6, 16, 128), F32),
    ((6, 16, 128), F32),
    ((1536, 128), F32),
    ((384, 512), BF),
    ((512, 384), F32),
]


def call(body, outs, cost, scratch=(), grid=None, in_specs=None, out_specs=None, vmem=16):
    params = {}
    if grid is not None:
        params = {"grid": grid, "in_specs": in_specs, "out_specs": out_specs}
    elif in_specs is not None:
        params = {"in_specs": in_specs}
        if out_specs is not None:
            params["out_specs"] = out_specs
    return pl.pallas_call(
        body,
        out_shape=outs,
        scratch_shapes=list(scratch),
        cost_estimate=pl.CostEstimate(flops=int(cost[0]), bytes_accessed=int(cost[1]), transcendentals=0),
        compiler_params=pltpu.CompilerParams(vmem_limit_bytes=vmem * 1024 * 1024),
        **params,
    )


def ones_where(cond):
    return jnp.where(cond, 1.0, 0.0).astype(BF)


def weight_body(me_ref, seg_ref, wt_ref, wide_ref, copy_ref, mask_ref, tall):
    me = me_ref[0]
    for b in range(2):
        for f in range(4):
            frame = (me >> 5) * 4 + f
            for a in range(3):
                before = frame - (2 - a)
                same = (before >= 0) & (seg_ref[b, jnp.maximum(before, 0)] == seg_ref[b, frame])
                mask_ref[12 * b + 3 * f + a] = jnp.where(same, 1, 0)
    copy_ref[...] = wt_ref[...]
    tall[0:432, :] = wt_ref[...].astype(F32)
    tall[432:512, :] = jnp.zeros((80, 384), F32)
    wide_ref[...] = (tall[...] * 0.5).T.astype(BF)


def select_body(me_ref, order_ref, send_ref, take_ref):
    me = me_ref[0]
    order = order_ref[...]
    mine = ((order >> 14) * 32 + ((order >> 7) & 31)) == me
    local_id = (((order >> 12) & 3) * 2 + ((order >> 6) & 1)) * 64 + (order & 63)
    hits = ones_where(mine)
    up = lax.broadcasted_iota(jnp.int32, (128, 128), 0)
    lane = lax.broadcasted_iota(jnp.int32, (128, 128), 1)
    running = matmul(hits, ones_where(up <= lane))
    row = lax.broadcasted_iota(jnp.int32, (512, 512), 0)
    col = lax.broadcasted_iota(jnp.int32, (512, 512), 1)
    group = (row >> 2) == (col >> 2)
    above = matmul(ones_where(group & (col < row)), hits)
    running = running + jnp.sum(above, axis=1, keepdims=True)
    lane = lax.broadcasted_iota(jnp.int32, (512, 128), 1)
    slot = lax.broadcasted_iota(jnp.int32, (512, 128), 0) & 3
    found = jnp.zeros((512, 128), F32)
    for s in range(4):
        hit = mine & (running == s + 1.0)
        high = jnp.sum(jnp.where(hit, local_id >> 4, 0).astype(F32), axis=1, keepdims=True)
        low = jnp.sum(jnp.where(hit, local_id & 15, 0).astype(F32), axis=1, keepdims=True)
        found = found + jnp.where(lane == s, high, 0.0) + jnp.where(lane == s + 4, low, 0.0)
    found = matmul(ones_where(group), found.astype(BF))
    found = jnp.where(lane == slot, found * 16.0, 0.0) + jnp.where(lane == slot + 4, found, 0.0)
    place = 2 * jnp.sum(found, axis=1, keepdims=True).astype(jnp.int32)
    send_ref[...] = jnp.broadcast_to(place, (512, 128))
    pair = order_ref[pl.ds(pl.multiple_of((me >> 1) * 8, 8), 8), :]
    four = jnp.where((me & 1) == 0, pair[0:4], pair[4:8])
    own = jnp.concatenate([four[i : i + 1] for i in range(4)], axis=1)
    sender = (own >> 14) * 32 + ((own >> 7) & 31)
    pos = lax.broadcasted_iota(jnp.int32, (256, 512), 1)
    half = lax.broadcasted_iota(jnp.int32, (256, 512), 0)
    for e in range(2):
        here = pos == 2 * half + e
        mate = jnp.sum(jnp.where(here, sender, 0).astype(F32), axis=1, keepdims=True).astype(jnp.int32)
        earlier = (sender == mate) & (pos < 2 * half + e)
        count = jnp.sum(jnp.where(earlier, 1.0, 0.0), axis=1, keepdims=True)
        far = jnp.where((mate & 1) == (me & 1), 0, 256)
        take_ref[e] = jnp.broadcast_to(far + (mate >> 1) * 4 + count.astype(jnp.int32), (256, 128))


def main_body(
    core_ref, mask_ref, prev, lat, near, far, cot_hbm, wide, wt, keep, pair, own, gfar, gprev,
    cot, ext, patch, pre, total, spread, edges, cots, grad, turned, cot_sems,
):
    lanes = lax.broadcasted_iota(jnp.int32, (1, 128), 1)
    near_row = 5 - 5 * core_ref[0]

    def cot_copy(i):
        return pltpu.make_async_copy(cot_hbm.at[i >> 2, :, i & 3], cot.at[i], cot_sems.at[i])

    for i in range(8):
        cot_copy(i).start()
    patch[432:512, :] = jnp.zeros((80, 512), BF)
    total[...] = jnp.zeros_like(total)
    spread[...] = jnp.zeros_like(spread)
    for b in range(2):
        for h in range(4):
            ext[b, 1, 0:2, 1 + h] = prev[h, b]
            ext[b, 1, 2:6, 1 + h] = lat[h, b]
        ext[b, 1, :, near_row] = near[b]
        ext[b, 1, :, 5 - near_row] = far[b]
        for fr in range(6):
            x = ext[b, 1, fr].astype(F32).reshape(96, 128)
            left = jnp.where(lanes == 0, 0.0, pltpu.roll(x, 1, 1))
            right = jnp.where(lanes == 127, 0.0, pltpu.roll(x, 127, 1))
            ext[b, 0, fr] = left.astype(BF).reshape(6, 16, 128)
            ext[b, 2, fr] = right.astype(BF).reshape(6, 16, 128)

    def factors(i):
        return [mask_ref[3 * i + a].astype(F32) for a in range(3)]

    def build(i):
        b, f = i >> 2, i & 3
        masks = factors(i)
        for a in range(3):
            mask = jnp.full((16, 128), masks[a], F32).astype(BF)
            for r in range(3):
                for c in range(3):
                    top = (a * 9 + r * 3 + c) * 16
                    for h in range(4):
                        patch[top : top + 16, h * 128 : h * 128 + 128] = ext[b, c, f + a, h + r] * mask

    def relayout(i):
        cot_copy(i).wait()
        cots[...] = cot[i].astype(F32).reshape(1536, 128)

    def elements(h):
        x = pre[:, h * 128 : h * 128 + 128]
        t = jnp.tanh(x)
        cot = cots[pl.ds(h, 384, stride=4), :]
        grad[:, h * 128 : h * 128 + 128] = (cot * (1.0 + t) * (1.0 + x * (1.0 - t))).astype(BF)

    def spread_tap(i, a, back):
        b, f = i >> 2, i & 3
        mask = factors(i)[a]
        for c in range(3):
            for row in range(6):
                acc = None
                for r in range(3):
                    h = row - r
                    if 0 <= h < 4:
                        top = (r * 3 + c) * 16
                        term = back[top : top + 16, h * 128 : h * 128 + 128]
                        acc = term if acc is None else acc + term
                spread[b, c, f + a, row] += acc * mask

    def step(i, carry):
        build(i)
        relayout(i)
        pre[...] = matmul(wide[...], patch[...])
        for h in range(4):
            elements(h)
        back = matmul(wt[...], grad[...])
        total[...] += matmul_nt(grad[...], patch[...])
        for a in range(3):
            spread_tap(i, a, back[a * 144 : a * 144 + 144])
        return carry

    lax.fori_loop(0, 8, step, 0)
    turned[...] = total[...].T
    mine = core_ref[0] * 256
    for g in range(16):
        for i in range(3):
            cols = slice(i * 128, i * 128 + 128)
            kept = pl.multiple_of(mine + g * 16, 16)
            pair[g * 3 + i] = turned[pl.ds(pl.multiple_of(256 - mine + g * 16, 16), 16), cols].astype(BF)
            keep[g * 3 + i] = turned[pl.ds(kept, 16), cols].astype(BF)
    for b in range(2):
        for fr in range(6):
            x0 = spread[b, 0, fr].reshape(96, 128)
            x2 = spread[b, 2, fr].reshape(96, 128)
            x = (
                spread[b, 1, fr].reshape(96, 128)
                + jnp.where(lanes == 127, 0.0, pltpu.roll(x0, 127, 1))
                + jnp.where(lanes == 0, 0.0, pltpu.roll(x2, 1, 1))
            ).reshape(6, 16, 128) * 0.5
            edges[0] = x[0]
            edges[5] = x[5]
            pair[48 + b * 6 + fr] = edges[near_row].astype(BF)
            gfar[b, fr] = edges[5 - near_row].astype(BF)
            if fr < 2:
                gprev[b, fr] = x[1:5]
            else:
                own[b, fr - 2] = x[1:5]


def mix_body(core_ref, keep_ref, given_ref, gprev_ref, far_ref, half_ref, early_ref):
    for g in range(16):
        for i in range(3):
            x = keep_ref[g * 3 + i].astype(F32) + given_ref[g * 3 + i].astype(F32)
            half_ref[g * 4 : g * 4 + 4, :, i * 128 : i * 128 + 128] = x.reshape(4, 4, 128).astype(BF)
    near_row = 3 - 3 * core_ref[0]
    early_ref[...] = gprev_ref[...].astype(BF)
    for b in range(2):
        for f in range(2):
            near = given_ref[48 + b * 6 + f].astype(F32)
            early_ref[b, f, near_row] = (gprev_ref[b, f, near_row] + near).astype(BF)
            far = far_ref[b, f].astype(F32)
            early_ref[b, f, 3 - near_row] = (gprev_ref[b, f, 3 - near_row] + far).astype(BF)


def out_body(core_ref, own_ref, given_ref, far_ref, next_ref, send_ref, part_ref, twin_ref, out_ref, rows, grad):
    near_row = 3 - 3 * core_ref[0]
    grad[...] = own_ref[...]
    for b in range(2):
        for f in range(4):
            grad[b, f, near_row] += given_ref[50 + b * 6 + f].astype(F32)
            grad[b, f, 3 - near_row] += far_ref[b, 2 + f].astype(F32)
            for h in range(4):
                x = grad[b, f, h]
                if f >= 2:
                    x = x + next_ref[b, f - 2, h].astype(F32)
                x = x.astype(BF)
                top = (b * 2 + h % 2) * 16
                col = (f * 2 + h // 2) * 128
                rows[top : top + 16, col : col + 128] = x
                rows[64 + top : 80 + top, col : col + 128] = pltpu.roll(x.astype(F32), 127, 1).astype(BF)
    place = send_ref[...]
    lane = lax.broadcasted_iota(jnp.int32, (512, 128), 1)
    send = jnp.concatenate([ones_where(place == lane + i * 128) for i in range(8)], axis=1)
    tokens = matmul_nt(send, rows[...]).reshape(64, 2, 4, 128)
    out_ref[:, 0:2] = tokens.astype(BF)
    part = (part_ref[...] + twin_ref[...]) * (0.5 / math.sqrt(4 * 16 * 128 * 128))
    for i in range(3):
        piece = part[:, i * 128 : i * 128 + 128].astype(BF)
        out_ref[:, 2 + i] = jnp.broadcast_to(piece[None], (64, 4, 128))


def take_body(core_ref, mine_ref, other_ref, take_ref, out_ref, wg_ref):
    core = core_ref[0]
    got = jnp.concatenate([ref[:, core].astype(F32).reshape(256, 128) for ref in (mine_ref, other_ref)]).astype(BF)
    src = lax.broadcasted_iota(jnp.int32, (128, 128), 0)
    dst = lax.broadcasted_iota(jnp.int32, (128, 128), 1)
    lane = lax.broadcasted_iota(jnp.int32, (256, 128), 1)
    want = ((dst & 1) << 6) + (((dst >> 1) & 1) << 4) + ((dst >> 2) & 15)
    takes = []
    for e in range(2):
        row = take_ref[e]
        takes.append(jnp.concatenate([ones_where(row == lane + i * 128) for i in range(4)], axis=1))
    for b in range(2):
        total = None
        for e in range(2):
            place = ones_where((src == want + b * 32) & ((dst >> 6) == e))
            moved = matmul(got, place).astype(BF)
            term = matmul(takes[e], moved)
            total = term if total is None else total + term
        out_ref[b] = total.astype(BF)
    for i in range(3):
        mine = mine_ref[:, 2 + i].astype(F32)
        other = other_ref[:, 2 + i].astype(F32)
        halves = (jnp.where(core == 0, mine, other), jnp.where(core == 0, other, mine))
        for c in range(2):
            for j in range(64):
                top = c * 256 + (j & 15) * 16 + (j >> 4) * 4
                if top < 432:
                    wg_ref[top : top + 4, i * 128 : i * 128 + 128] = halves[c][j]


def shifted(value, step):
    count = lax.axis_size("tm")
    return lax.ppermute(value, "tm", [(i, i + step) for i in range(count) if 0 <= i + step < count])


def crossed(value):
    count = math.prod(lax.axis_size(a) for a in BAND)
    pairs = [(i, i + 1) for i in range(1, count - 1, 2)]
    return lax.ppermute(value, BAND, pairs + [(j, i) for i, j in pairs])


def swapped(value):
    return lax.ppermute(value, "core", [(0, 1), (1, 0)])


def exchange(value, axes):
    return lax.all_to_all(value, axes, split_axis=0, concat_axis=0, tiled=True)


def whole(shape):
    return pl.BlockSpec(shape, lambda b, f: (0,) * len(shape))


def on_device(latent, weight, cotangent, groups, order):
    tm = lax.axis_index("tm")
    core = lax.axis_index("core")
    me = tm * 32 + lax.axis_index(BAND)
    smem = pl.BlockSpec(memory_space=pltpu.SMEM)
    vmem = pl.BlockSpec(memory_space=pltpu.VMEM)
    hbm = pl.BlockSpec(memory_space=pltpu.HBM)
    lat = latent.transpose(3, 0, 2, 1, 4)
    prev = shifted(lat[:, :, 2:4], 1)
    wide, tall, masks = call(
        weight_body,
        (
            jax.ShapeDtypeStruct((384, 512), BF),
            jax.ShapeDtypeStruct((432, 384), BF),
            jax.ShapeDtypeStruct((24,), jnp.int32),
        ),
        (1e6, 2e6),
        scratch=[pltpu.VMEM((512, 384), F32)],
        in_specs=[smem, smem, vmem],
        out_specs=[vmem] * 2 + [smem],
        vmem=52,
    )(me.reshape(1), groups, weight.T)
    prev, masks = lax.optimization_barrier((prev, masks))
    edge = lambda row: jnp.concatenate([lax.dynamic_index_in_dim(x, row, 0, False) for x in (prev, lat)], axis=1)
    far = crossed(edge(3 * core))
    near = swapped(edge(3 - 3 * core))
    send, take = call(
        select_body,
        (jax.ShapeDtypeStruct((512, 128), jnp.int32), jax.ShapeDtypeStruct((2, 256, 128), jnp.int32)),
        (500e6, 2e6),
        in_specs=[smem, vmem],
        out_specs=[vmem] * 2,
        vmem=52,
    )(me.reshape(1), order.reshape(512, 128))
    far, send = lax.optimization_barrier((far, send))
    keep, pair, grad, gfar, gprev = call(
        main_body,
        tuple(jax.ShapeDtypeStruct(*out) for out in MAIN_OUTS),
        (4.5e9, 5e6),
        scratch=[pltpu.VMEM(*x) for x in MAIN_SCRATCH] + [pltpu.SemaphoreType.DMA((8,))],
        in_specs=[smem, smem] + [vmem] * 4 + [hbm] + [vmem] * 2,
        out_specs=[vmem] * 5,
        vmem=52,
    )(core.reshape(1), masks, prev, lat, near, far, cotangent, wide, tall)
    from_far = crossed(gfar)
    given = swapped(pair)
    half, early = call(
        mix_body,
        (jax.ShapeDtypeStruct((64, 4, 384), BF), jax.ShapeDtypeStruct((2, 2, 4, 16, 128), BF)),
        (1e5, 1e6),
        in_specs=[smem] + [vmem] * 4,
    )(core.reshape(1), keep, given, gprev, from_far)
    from_next = shifted(early, -1)
    parts = exchange(half, CHIPS)
    part = jnp.sum(parts.astype(F32), axis=0)
    twin = lax.ppermute(part, "rep", [(0, 1), (1, 0)])
    outgoing = call(
        out_body,
        jax.ShapeDtypeStruct((64, 5, 4, 128), BF),
        (150e6, 2e6),
        scratch=[pltpu.VMEM((128, 1024), BF), pltpu.VMEM((2, 4, 4, 16, 128), F32)],
        in_specs=[smem] + [vmem] * 7,
    )(core.reshape(1), grad, given, from_far, from_next, send, part, twin)
    got = exchange(outgoing, ("tm", "xl", "z"))
    other = swapped(got)
    tokens, summed = call(
        take_body,
        (jax.ShapeDtypeStruct((2, 256, 128), BF), jax.ShapeDtypeStruct((432, 384), F32)),
        (200e6, 1e6),
        in_specs=[smem] + [vmem] * 3,
    )(core.reshape(1), got, other, take)
    return tokens, summed.T


def solution(mesh):
    split = Mesh(mesh.devices.reshape(4, 2, 8, 2, 2), ("tm", "xl", "z", "core", "rep"))
    placed = P("rep", None, "tm", BAND, None)
    return jax.shard_map(
        on_device,
        mesh=split,
        in_specs=(placed, P(), placed, P("rep", None), P()),
        out_specs=(P("rep", PEERS, None), P()),
        check_vma=False,
    )
```

```python
import math

import jax
import jax.numpy as jnp
from jax import lax
from jax.experimental import pallas as pl
from jax.experimental.pallas import tpu as pltpu
from jax.sharding import Mesh, PartitionSpec as P

BF = jnp.bfloat16
F32 = jnp.float32
BAND = ("xl", "z", "core")
PEERS = ("tm", "xl", "z", "core")
CHIPS = ("xl", "z", "tm")
NT = (((1,), (1,)), ((), ()))


def matmul(a, b):
    return jnp.dot(a, b, preferred_element_type=F32)


def matmul_nt(a, b):
    return lax.dot_general(a, b, NT, preferred_element_type=F32)


MAIN_OUTS = [
    ((48, 16, 128), BF),
    ((60, 16, 128), BF),
    ((2, 4, 4, 16, 128), F32),
    ((2, 6, 16, 128), BF),
    ((2, 2, 4, 16, 128), F32),
]
MAIN_SCRATCH = [
    ((8, 384, 4, 128), BF),
    ((2, 3, 6, 6, 16, 128), BF),
    ((512, 512), BF),
    ((384, 512), F32),
    ((384, 512), F32),
    ((2, 3, 6, 6, 16, 128), F32),
    ((6, 16, 128), F32),
    ((1536, 128), F32),
    ((384, 512), BF),
    ((512, 384), F32),
    ((512, 512), BF),
    ((384, 512), F32),
]


def call(body, outs, cost, scratch=(), grid=None, in_specs=None, out_specs=None, vmem=16):
    params = {}
    if grid is not None:
        params = {"grid": grid, "in_specs": in_specs, "out_specs": out_specs}
    elif in_specs is not None:
        params = {"in_specs": in_specs}
        if out_specs is not None:
            params["out_specs"] = out_specs
    return pl.pallas_call(
        body,
        out_shape=outs,
        scratch_shapes=list(scratch),
        cost_estimate=pl.CostEstimate(flops=int(cost[0]), bytes_accessed=int(cost[1]), transcendentals=0),
        compiler_params=pltpu.CompilerParams(vmem_limit_bytes=vmem * 1024 * 1024),
        **params,
    )


def ones_where(cond):
    return jnp.where(cond, 1.0, 0.0).astype(BF)


def weight_body(me_ref, seg_ref, wt_ref, wide_ref, copy_ref, mask_ref, tall):
    me = me_ref[0]
    for b in range(2):
        for f in range(4):
            frame = (me >> 5) * 4 + f
            for a in range(3):
                before = frame - (2 - a)
                same = (before >= 0) & (seg_ref[b, jnp.maximum(before, 0)] == seg_ref[b, frame])
                mask_ref[12 * b + 3 * f + a] = jnp.where(same, 1, 0)
    copy_ref[...] = wt_ref[...]
    tall[0:432, :] = wt_ref[...].astype(F32)
    tall[432:512, :] = jnp.zeros((80, 384), F32)
    wide_ref[...] = (tall[...] * 0.5).T.astype(BF)


def select_body(me_ref, order_ref, send_ref, take_ref):
    me = me_ref[0]
    order = order_ref[...]
    mine = ((order >> 14) * 32 + ((order >> 7) & 31)) == me
    local_id = (((order >> 12) & 3) * 2 + ((order >> 6) & 1)) * 64 + (order & 63)
    hits = ones_where(mine)
    up = lax.broadcasted_iota(jnp.int32, (128, 128), 0)
    lane = lax.broadcasted_iota(jnp.int32, (128, 128), 1)
    running = matmul(hits, ones_where(up <= lane))
    row = lax.broadcasted_iota(jnp.int32, (512, 512), 0)
    col = lax.broadcasted_iota(jnp.int32, (512, 512), 1)
    group = (row >> 2) == (col >> 2)
    above = matmul(ones_where(group & (col < row)), hits)
    running = running + jnp.sum(above, axis=1, keepdims=True)
    lane = lax.broadcasted_iota(jnp.int32, (512, 128), 1)
    slot = lax.broadcasted_iota(jnp.int32, (512, 128), 0) & 3
    found = jnp.zeros((512, 128), F32)
    for s in range(4):
        hit = mine & (running == s + 1.0)
        high = jnp.sum(jnp.where(hit, local_id >> 4, 0).astype(F32), axis=1, keepdims=True)
        low = jnp.sum(jnp.where(hit, local_id & 15, 0).astype(F32), axis=1, keepdims=True)
        found = found + jnp.where(lane == s, high, 0.0) + jnp.where(lane == s + 4, low, 0.0)
    found = matmul(ones_where(group), found.astype(BF))
    found = jnp.where(lane == slot, found * 16.0, 0.0) + jnp.where(lane == slot + 4, found, 0.0)
    place = 2 * jnp.sum(found, axis=1, keepdims=True).astype(jnp.int32)
    send_ref[...] = jnp.broadcast_to(place, (512, 128))
    pair = order_ref[pl.ds(pl.multiple_of((me >> 1) * 8, 8), 8), :]
    four = jnp.where((me & 1) == 0, pair[0:4], pair[4:8])
    own = jnp.concatenate([four[i : i + 1] for i in range(4)], axis=1)
    sender = (own >> 14) * 32 + ((own >> 7) & 31)
    pos = lax.broadcasted_iota(jnp.int32, (256, 512), 1)
    half = lax.broadcasted_iota(jnp.int32, (256, 512), 0)
    for e in range(2):
        here = pos == 2 * half + e
        mate = jnp.sum(jnp.where(here, sender, 0).astype(F32), axis=1, keepdims=True).astype(jnp.int32)
        earlier = (sender == mate) & (pos < 2 * half + e)
        count = jnp.sum(jnp.where(earlier, 1.0, 0.0), axis=1, keepdims=True)
        far = jnp.where((mate & 1) == (me & 1), 0, 256)
        take_ref[e] = jnp.broadcast_to(far + (mate >> 1) * 4 + count.astype(jnp.int32), (256, 128))


def main_body(
    core_ref, mask_ref, prev, lat, near, far, cot_hbm, wide, wt, keep, pair, own, gfar, gprev,
    cot, ext, patch, pre, total, spread, edges, cots, grad, turned, patch1, pre1, cot_sems,
):
    lanes = lax.broadcasted_iota(jnp.int32, (1, 128), 1)
    near_row = 5 - 5 * core_ref[0]

    def cot_copy(i):
        return pltpu.make_async_copy(cot_hbm.at[i >> 2, :, i & 3], cot.at[i], cot_sems.at[i])

    for i in range(8):
        cot_copy(i).start()
    patch[432:512, :] = jnp.zeros((80, 512), BF)
    patch1[432:512, :] = jnp.zeros((80, 512), BF)
    total[...] = jnp.zeros_like(total)
    spread[...] = jnp.zeros_like(spread)
    for b in range(2):
        for h in range(4):
            ext[b, 1, 0:2, 1 + h] = prev[h, b]
            ext[b, 1, 2:6, 1 + h] = lat[h, b]
        ext[b, 1, :, near_row] = near[b]
        ext[b, 1, :, 5 - near_row] = far[b]
        for fr in range(6):
            x = ext[b, 1, fr].astype(F32).reshape(96, 128)
            left = jnp.where(lanes == 0, 0.0, pltpu.roll(x, 1, 1))
            right = jnp.where(lanes == 127, 0.0, pltpu.roll(x, 127, 1))
            ext[b, 0, fr] = left.astype(BF).reshape(6, 16, 128)
            ext[b, 2, fr] = right.astype(BF).reshape(6, 16, 128)

    def factors(i):
        return [mask_ref[3 * i + a].astype(F32) for a in range(3)]

    def build(i, patch):
        b, f = i >> 2, i & 3
        masks = factors(i)
        for a in range(3):
            mask = jnp.full((16, 128), masks[a], F32).astype(BF)
            for r in range(3):
                for c in range(3):
                    top = (a * 9 + r * 3 + c) * 16
                    for h in range(4):
                        patch[top : top + 16, h * 128 : h * 128 + 128] = ext[b, c, f + a, h + r] * mask

    def relayout(i):
        cot_copy(i).wait()
        cots[...] = cot[i].astype(F32).reshape(1536, 128)

    def elements(h, pre):
        x = pre[:, h * 128 : h * 128 + 128]
        t = jnp.tanh(x)
        cot = cots[pl.ds(h, 384, stride=4), :]
        grad[:, h * 128 : h * 128 + 128] = (cot * (1.0 + t) * (1.0 + x * (1.0 - t))).astype(BF)

    def spread_tap(i, a, back):
        b, f = i >> 2, i & 3
        mask = factors(i)[a]
        for c in range(3):
            for row in range(6):
                acc = None
                for r in range(3):
                    h = row - r
                    if 0 <= h < 4:
                        top = (r * 3 + c) * 16
                        term = back[top : top + 16, h * 128 : h * 128 + 128]
                        acc = term if acc is None else acc + term
                spread[b, c, f + a, row] += acc * mask

    def advance(i, patch, pre, next_patch, next_pre):
        build(jnp.minimum(i + 1, 7), next_patch)
        relayout(i)
        next_pre[...] = matmul(wide[...], next_patch[...])
        for h in range(4):
            elements(h, pre)
        back = matmul(wt[...], grad[...])
        total[...] += matmul_nt(grad[...], patch[...])
        for a in range(3):
            spread_tap(i, a, back[a * 144 : a * 144 + 144])

    build(0, patch)
    pre[...] = matmul(wide[...], patch[...])

    def step(j, carry):
        advance(2 * j, patch, pre, patch1, pre1)
        advance(2 * j + 1, patch1, pre1, patch, pre)
        return carry

    lax.fori_loop(0, 4, step, 0)
    turned[...] = total[...].T
    mine = core_ref[0] * 256
    for g in range(16):
        for i in range(3):
            cols = slice(i * 128, i * 128 + 128)
            kept = pl.multiple_of(mine + g * 16, 16)
            pair[g * 3 + i] = turned[pl.ds(pl.multiple_of(256 - mine + g * 16, 16), 16), cols].astype(BF)
            keep[g * 3 + i] = turned[pl.ds(kept, 16), cols].astype(BF)
    for b in range(2):
        for fr in range(6):
            x0 = spread[b, 0, fr].reshape(96, 128)
            x2 = spread[b, 2, fr].reshape(96, 128)
            x = (
                spread[b, 1, fr].reshape(96, 128)
                + jnp.where(lanes == 127, 0.0, pltpu.roll(x0, 127, 1))
                + jnp.where(lanes == 0, 0.0, pltpu.roll(x2, 1, 1))
            ).reshape(6, 16, 128) * 0.5
            edges[0] = x[0]
            edges[5] = x[5]
            pair[48 + b * 6 + fr] = edges[near_row].astype(BF)
            gfar[b, fr] = edges[5 - near_row].astype(BF)
            if fr < 2:
                gprev[b, fr] = x[1:5]
            else:
                own[b, fr - 2] = x[1:5]


def add_body(keep_ref, given_ref, out_ref):
    for g in range(16):
        for i in range(3):
            x = keep_ref[g * 3 + i].astype(F32) + given_ref[g * 3 + i].astype(F32)
            out_ref[g * 4 : g * 4 + 4, :, i * 128 : i * 128 + 128] = x.reshape(4, 4, 128).astype(BF)


def early_body(core_ref, gprev_ref, given_ref, far_ref, out_ref):
    near_row = 3 - 3 * core_ref[0]
    out_ref[...] = gprev_ref[...].astype(BF)
    for b in range(2):
        for f in range(2):
            near = given_ref[48 + b * 6 + f].astype(F32)
            out_ref[b, f, near_row] = (gprev_ref[b, f, near_row] + near).astype(BF)
            far = far_ref[b, f].astype(F32)
            out_ref[b, f, 3 - near_row] = (gprev_ref[b, f, 3 - near_row] + far).astype(BF)


def out_body(core_ref, own_ref, given_ref, far_ref, next_ref, send_ref, part_ref, twin_ref, out_ref, rows, grad):
    near_row = 3 - 3 * core_ref[0]
    grad[...] = own_ref[...]
    for b in range(2):
        for f in range(4):
            grad[b, f, near_row] += given_ref[50 + b * 6 + f].astype(F32)
            grad[b, f, 3 - near_row] += far_ref[b, 2 + f].astype(F32)
            for h in range(4):
                x = grad[b, f, h]
                if f >= 2:
                    x = x + next_ref[b, f - 2, h].astype(F32)
                x = x.astype(BF)
                top = (b * 2 + h % 2) * 16
                col = (f * 2 + h // 2) * 128
                rows[top : top + 16, col : col + 128] = x
                rows[64 + top : 80 + top, col : col + 128] = pltpu.roll(x.astype(F32), 127, 1).astype(BF)
    place = send_ref[...]
    lane = lax.broadcasted_iota(jnp.int32, (512, 128), 1)
    send = jnp.concatenate([ones_where(place == lane + i * 128) for i in range(8)], axis=1)
    tokens = matmul_nt(send, rows[...]).reshape(64, 2, 4, 128)
    out_ref[:, 0:2] = tokens.astype(BF)
    part = (part_ref[...] + twin_ref[...]) * (0.5 / math.sqrt(4 * 16 * 128 * 128))
    for i in range(3):
        piece = part[:, i * 128 : i * 128 + 128].astype(BF)
        out_ref[:, 2 + i] = jnp.broadcast_to(piece[None], (64, 4, 128))


def take_body(core_ref, mine_ref, other_ref, take_ref, out_ref, wg_ref):
    core = core_ref[0]
    got = jnp.concatenate([ref[:, core].astype(F32).reshape(256, 128) for ref in (mine_ref, other_ref)]).astype(BF)
    src = lax.broadcasted_iota(jnp.int32, (128, 128), 0)
    dst = lax.broadcasted_iota(jnp.int32, (128, 128), 1)
    lane = lax.broadcasted_iota(jnp.int32, (256, 128), 1)
    want = ((dst & 1) << 6) + (((dst >> 1) & 1) << 4) + ((dst >> 2) & 15)
    takes = []
    for e in range(2):
        row = take_ref[e]
        takes.append(jnp.concatenate([ones_where(row == lane + i * 128) for i in range(4)], axis=1))
    for b in range(2):
        total = None
        for e in range(2):
            place = ones_where((src == want + b * 32) & ((dst >> 6) == e))
            moved = matmul(got, place).astype(BF)
            term = matmul(takes[e], moved)
            total = term if total is None else total + term
        out_ref[b] = total.astype(BF)
    for i in range(3):
        mine = mine_ref[:, 2 + i].astype(F32)
        other = other_ref[:, 2 + i].astype(F32)
        halves = (jnp.where(core == 0, mine, other), jnp.where(core == 0, other, mine))
        for c in range(2):
            for j in range(64):
                top = c * 256 + (j & 15) * 16 + (j >> 4) * 4
                if top < 432:
                    wg_ref[top : top + 4, i * 128 : i * 128 + 128] = halves[c][j]


def shifted(value, step):
    count = lax.axis_size("tm")
    return lax.ppermute(value, "tm", [(i, i + step) for i in range(count) if 0 <= i + step < count])


def crossed(value):
    count = math.prod(lax.axis_size(a) for a in BAND)
    pairs = [(i, i + 1) for i in range(1, count - 1, 2)]
    return lax.ppermute(value, BAND, pairs + [(j, i) for i, j in pairs])


def swapped(value):
    return lax.ppermute(value, "core", [(0, 1), (1, 0)])


def exchange(value, axes):
    return lax.all_to_all(value, axes, split_axis=0, concat_axis=0, tiled=True)


def whole(shape):
    return pl.BlockSpec(shape, lambda b, f: (0,) * len(shape))


def on_device(latent, weight, cotangent, groups, order):
    tm = lax.axis_index("tm")
    core = lax.axis_index("core")
    me = tm * 32 + lax.axis_index(BAND)
    smem = pl.BlockSpec(memory_space=pltpu.SMEM)
    vmem = pl.BlockSpec(memory_space=pltpu.VMEM)
    hbm = pl.BlockSpec(memory_space=pltpu.HBM)
    lat = latent.transpose(3, 0, 2, 1, 4)
    prev = shifted(lat[:, :, 2:4], 1)
    wide, tall, masks = call(
        weight_body,
        (
            jax.ShapeDtypeStruct((384, 512), BF),
            jax.ShapeDtypeStruct((432, 384), BF),
            jax.ShapeDtypeStruct((24,), jnp.int32),
        ),
        (1e6, 2e6),
        scratch=[pltpu.VMEM((512, 384), F32)],
        in_specs=[smem, smem, vmem],
        out_specs=[vmem] * 2 + [smem],
        vmem=52,
    )(me.reshape(1), groups, weight.T)
    prev, masks = lax.optimization_barrier((prev, masks))
    edge = lambda row: jnp.concatenate([lax.dynamic_index_in_dim(x, row, 0, False) for x in (prev, lat)], axis=1)
    far = crossed(edge(3 * core))
    near = swapped(edge(3 - 3 * core))
    send, take = call(
        select_body,
        (jax.ShapeDtypeStruct((512, 128), jnp.int32), jax.ShapeDtypeStruct((2, 256, 128), jnp.int32)),
        (500e6, 2e6),
        in_specs=[smem, vmem],
        out_specs=[vmem] * 2,
        vmem=52,
    )(me.reshape(1), order.reshape(512, 128))
    far, send = lax.optimization_barrier((far, send))
    keep, pair, grad, gfar, gprev = call(
        main_body,
        tuple(jax.ShapeDtypeStruct(*out) for out in MAIN_OUTS),
        (4.5e9, 5e6),
        scratch=[pltpu.VMEM(*x) for x in MAIN_SCRATCH] + [pltpu.SemaphoreType.DMA((8,))],
        in_specs=[smem, smem] + [vmem] * 4 + [hbm] + [vmem] * 2,
        out_specs=[vmem] * 5,
        vmem=52,
    )(core.reshape(1), masks, prev, lat, near, far, cotangent, wide, tall)
    from_far = crossed(gfar)
    given = swapped(pair)
    half = call(add_body, jax.ShapeDtypeStruct((64, 4, 384), BF), (1e5, 3e7), in_specs=[vmem] * 2)(keep, given)
    early = call(
        early_body,
        jax.ShapeDtypeStruct((2, 2, 4, 16, 128), BF),
        (1e5, 3e5),
        in_specs=[smem] + [vmem] * 3,
    )(core.reshape(1), gprev, given, from_far)
    from_next = shifted(early, -1)
    parts = exchange(half, CHIPS)
    part = jnp.sum(parts.astype(F32), axis=0)
    twin = lax.ppermute(part, "rep", [(0, 1), (1, 0)])
    outgoing = call(
        out_body,
        jax.ShapeDtypeStruct((64, 5, 4, 128), BF),
        (150e6, 2e6),
        scratch=[pltpu.VMEM((128, 1024), BF), pltpu.VMEM((2, 4, 4, 16, 128), F32)],
        in_specs=[smem] + [vmem] * 7,
    )(core.reshape(1), grad, given, from_far, from_next, send, part, twin)
    got = exchange(outgoing, ("tm", "xl", "z"))
    other = swapped(got)
    tokens, summed = call(
        take_body,
        (jax.ShapeDtypeStruct((2, 256, 128), BF), jax.ShapeDtypeStruct((432, 384), F32)),
        (200e6, 1e6),
        in_specs=[smem] + [vmem] * 3,
    )(core.reshape(1), got, other, take)
    return tokens, summed.T


def solution(mesh):
    split = Mesh(mesh.devices.reshape(4, 2, 8, 2, 2), ("tm", "xl", "z", "core", "rep"))
    placed = P("rep", None, "tm", BAND, None)
    return jax.shard_map(
        on_device,
        mesh=split,
        in_specs=(placed, P(), placed, P("rep", None), P()),
        out_specs=(P("rep", PEERS, None), P()),
        check_vma=False,
    )
```

```python
import math

import jax
import jax.numpy as jnp
from jax import lax
from jax.experimental import pallas as pl
from jax.experimental.pallas import tpu as pltpu
from jax.sharding import Mesh, PartitionSpec as P

BF = jnp.bfloat16
F32 = jnp.float32
BAND = ("xl", "z", "core")
PEERS = ("tm", "xl", "z", "core")
CHIPS = ("tm", "xl", "z")
NT = (((1,), (1,)), ((), ()))


def matmul(a, b):
    return jnp.dot(a, b, preferred_element_type=F32)


def matmul_nt(a, b):
    return lax.dot_general(a, b, NT, preferred_element_type=F32)


MAIN_OUTS = [
    ((48, 16, 128), BF),
    ((60, 16, 128), BF),
    ((2, 4, 4, 16, 128), F32),
    ((2, 6, 16, 128), BF),
    ((2, 2, 4, 16, 128), F32),
]
MAIN_SCRATCH = [
    ((8, 384, 4, 128), BF),
    ((2, 3, 6, 6, 16, 128), BF),
    ((512, 512), BF),
    ((384, 512), F32),
    ((384, 512), F32),
    ((2, 3, 6, 6, 16, 128), F32),
    ((6, 16, 128), F32),
    ((1544, 128), F32),
    ((384, 512), BF),
    ((512, 384), F32),
    ((512, 512), BF),
    ((384, 512), F32),
]


def call(body, outs, cost, scratch=(), grid=None, in_specs=None, out_specs=None, vmem=16):
    params = {}
    if grid is not None:
        params = {"grid": grid, "in_specs": in_specs, "out_specs": out_specs}
    elif in_specs is not None:
        params = {"in_specs": in_specs}
        if out_specs is not None:
            params["out_specs"] = out_specs
    return pl.pallas_call(
        body,
        out_shape=outs,
        scratch_shapes=list(scratch),
        cost_estimate=pl.CostEstimate(flops=int(cost[0]), bytes_accessed=int(cost[1]), transcendentals=0),
        compiler_params=pltpu.CompilerParams(vmem_limit_bytes=vmem * 1024 * 1024),
        **params,
    )


def ones_where(cond):
    return jnp.where(cond, 1.0, 0.0).astype(BF)


def weight_body(me_ref, seg_ref, wt_ref, wide_ref, copy_ref, mask_ref, tall):
    me = me_ref[0]
    for b in range(2):
        for f in range(4):
            frame = (me >> 5) * 4 + f
            for a in range(3):
                before = frame - (2 - a)
                same = (before >= 0) & (seg_ref[b, jnp.maximum(before, 0)] == seg_ref[b, frame])
                mask_ref[12 * b + 3 * f + a] = jnp.where(same, 1, 0)
    copy_ref[...] = wt_ref[...]
    tall[0:432, :] = wt_ref[...].astype(F32)
    tall[432:512, :] = jnp.zeros((80, 384), F32)
    wide_ref[...] = (tall[...] * 0.5).T.astype(BF)


def select_body(me_ref, order_ref, send_ref, take_ref):
    me = me_ref[0]
    order = order_ref[...]
    mine = ((order >> 14) * 32 + ((order >> 7) & 31)) == me
    local_id = (((order >> 12) & 3) * 2 + ((order >> 6) & 1)) * 64 + (order & 63)
    hits = ones_where(mine)
    up = lax.broadcasted_iota(jnp.int32, (128, 128), 0)
    lane = lax.broadcasted_iota(jnp.int32, (128, 128), 1)
    running = matmul(hits, ones_where(up <= lane))
    row = lax.broadcasted_iota(jnp.int32, (512, 512), 0)
    col = lax.broadcasted_iota(jnp.int32, (512, 512), 1)
    group = (row >> 2) == (col >> 2)
    above = matmul(ones_where(group & (col < row)), hits)
    running = running + jnp.sum(above, axis=1, keepdims=True)
    lane = lax.broadcasted_iota(jnp.int32, (512, 128), 1)
    slot = lax.broadcasted_iota(jnp.int32, (512, 128), 0) & 3
    found = jnp.zeros((512, 128), F32)
    for s in range(4):
        hit = mine & (running == s + 1.0)
        high = jnp.sum(jnp.where(hit, local_id >> 4, 0).astype(F32), axis=1, keepdims=True)
        low = jnp.sum(jnp.where(hit, local_id & 15, 0).astype(F32), axis=1, keepdims=True)
        found = found + jnp.where(lane == s, high, 0.0) + jnp.where(lane == s + 4, low, 0.0)
    found = matmul(ones_where(group), found.astype(BF))
    found = jnp.where(lane == slot, found * 16.0, 0.0) + jnp.where(lane == slot + 4, found, 0.0)
    place = 2 * jnp.sum(found, axis=1, keepdims=True).astype(jnp.int32)
    send_ref[...] = jnp.broadcast_to(place, (512, 128))
    pair = order_ref[pl.ds(pl.multiple_of((me >> 1) * 8, 8), 8), :]
    four = jnp.where((me & 1) == 0, pair[0:4], pair[4:8])
    own = jnp.concatenate([four[i : i + 1] for i in range(4)], axis=1)
    sender = (own >> 14) * 32 + ((own >> 7) & 31)
    pos = lax.broadcasted_iota(jnp.int32, (256, 512), 1)
    half = lax.broadcasted_iota(jnp.int32, (256, 512), 0)
    for e in range(2):
        here = pos == 2 * half + e
        mate = jnp.sum(jnp.where(here, sender, 0).astype(F32), axis=1, keepdims=True).astype(jnp.int32)
        earlier = (sender == mate) & (pos < 2 * half + e)
        count = jnp.sum(jnp.where(earlier, 1.0, 0.0), axis=1, keepdims=True)
        far = jnp.where((mate & 1) == (me & 1), 0, 256)
        take_ref[e] = jnp.broadcast_to(far + (mate >> 1) * 4 + count.astype(jnp.int32), (256, 128))


def main_body(
    core_ref, mask_ref, prev, lat, near, far, cot_hbm, wide, wt, keep, pair, own, gfar, gprev,
    cot, ext, patch, pre, total, spread, edges, cots, grad, turned, patch1, pre1, cot_sems,
):
    lanes = lax.broadcasted_iota(jnp.int32, (1, 128), 1)
    near_row = 5 - 5 * core_ref[0]

    def cot_copy(i):
        return pltpu.make_async_copy(cot_hbm.at[i >> 2, :, i & 3], cot.at[i], cot_sems.at[i])

    for i in range(8):
        cot_copy(i).start()
    patch[432:512, :] = jnp.zeros((80, 512), BF)
    patch1[432:512, :] = jnp.zeros((80, 512), BF)
    total[...] = jnp.zeros_like(total)
    spread[...] = jnp.zeros_like(spread)
    for b in range(2):
        for h in range(4):
            ext[b, 1, 0:2, 1 + h] = prev[h, b]
            ext[b, 1, 2:6, 1 + h] = lat[h, b]
        ext[b, 1, :, near_row] = near[b]
        ext[b, 1, :, 5 - near_row] = far[b]
        for fr in range(6):
            x = ext[b, 1, fr].astype(F32).reshape(96, 128)
            left = jnp.where(lanes == 0, 0.0, pltpu.roll(x, 1, 1))
            right = jnp.where(lanes == 127, 0.0, pltpu.roll(x, 127, 1))
            ext[b, 0, fr] = left.astype(BF).reshape(6, 16, 128)
            ext[b, 2, fr] = right.astype(BF).reshape(6, 16, 128)

    def factors(i):
        return [mask_ref[3 * i + a].astype(F32) for a in range(3)]

    def build(i, patch):
        b, f = i >> 2, i & 3
        masks = factors(i)
        for a in range(3):
            mask = jnp.full((16, 128), masks[a], F32).astype(BF)
            for r in range(3):
                for c in range(3):
                    top = (a * 9 + r * 3 + c) * 16
                    for h in range(4):
                        patch[top : top + 16, h * 128 : h * 128 + 128] = ext[b, c, f + a, h + r] * mask

    def relayout(i):
        cot_copy(i).wait()
        cots[0:1536] = cot[i].astype(F32).reshape(1536, 128)

    def elements(h, pre):
        x = pre[:, h * 128 : h * 128 + 128]
        t = jnp.tanh(x)
        cot = cots[pl.ds(h, 384, stride=4), :]
        grad[:, h * 128 : h * 128 + 128] = (cot * (1.0 + t) * (1.0 + x * (1.0 - t))).astype(BF)

    def spread_tap(i, a, back):
        b, f = i >> 2, i & 3
        mask = factors(i)[a]
        for c in range(3):
            for row in range(6):
                acc = None
                for r in range(3):
                    h = row - r
                    if 0 <= h < 4:
                        top = (r * 3 + c) * 16
                        term = back[top : top + 16, h * 128 : h * 128 + 128]
                        acc = term if acc is None else acc + term
                spread[b, c, f + a, row] += acc * mask

    def advance(i, patch, pre, next_patch, next_pre):
        build(jnp.minimum(i + 1, 7), next_patch)
        relayout(i)
        next_pre[...] = matmul(wide[...], next_patch[...])
        for h in range(4):
            elements(h, pre)
        back = matmul(wt[...], grad[...])
        total[...] += matmul_nt(grad[...], patch[...])
        for a in range(3):
            spread_tap(i, a, back[a * 144 : a * 144 + 144])

    build(0, patch)
    pre[...] = matmul(wide[...], patch[...])

    def step(j, carry):
        advance(2 * j, patch, pre, patch1, pre1)
        advance(2 * j + 1, patch1, pre1, patch, pre)
        return carry

    lax.fori_loop(0, 4, step, 0)
    turned[...] = total[...].T
    mine = core_ref[0] * 256
    for g in range(16):
        for i in range(3):
            cols = slice(i * 128, i * 128 + 128)
            kept = pl.multiple_of(mine + g * 16, 16)
            pair[g * 3 + i] = turned[pl.ds(pl.multiple_of(256 - mine + g * 16, 16), 16), cols].astype(BF)
            keep[g * 3 + i] = turned[pl.ds(kept, 16), cols].astype(BF)
    for b in range(2):
        for fr in range(6):
            x0 = spread[b, 0, fr].reshape(96, 128)
            x2 = spread[b, 2, fr].reshape(96, 128)
            x = (
                spread[b, 1, fr].reshape(96, 128)
                + jnp.where(lanes == 127, 0.0, pltpu.roll(x0, 127, 1))
                + jnp.where(lanes == 0, 0.0, pltpu.roll(x2, 1, 1))
            ).reshape(6, 16, 128) * 0.5
            edges[0] = x[0]
            edges[5] = x[5]
            pair[48 + b * 6 + fr] = edges[near_row].astype(BF)
            gfar[b, fr] = edges[5 - near_row].astype(BF)
            if fr < 2:
                gprev[b, fr] = x[1:5]
            else:
                own[b, fr - 2] = x[1:5]


def add_body(keep_ref, given_ref, out_ref):
    for g in range(16):
        for i in range(3):
            x = keep_ref[g * 3 + i].astype(F32) + given_ref[g * 3 + i].astype(F32)
            out_ref[g * 4 : g * 4 + 4, :, i * 128 : i * 128 + 128] = x.reshape(4, 4, 128).astype(BF)


def early_body(core_ref, gprev_ref, given_ref, far_ref, out_ref):
    near_row = 3 - 3 * core_ref[0]
    out_ref[...] = gprev_ref[...].astype(BF)
    for b in range(2):
        for f in range(2):
            near = given_ref[48 + b * 6 + f].astype(F32)
            out_ref[b, f, near_row] = (gprev_ref[b, f, near_row] + near).astype(BF)
            far = far_ref[b, f].astype(F32)
            out_ref[b, f, 3 - near_row] = (gprev_ref[b, f, 3 - near_row] + far).astype(BF)


def out_body(core_ref, own_ref, given_ref, far_ref, next_ref, send_ref, part_ref, twin_ref, out_ref, rows, grad):
    near_row = 3 - 3 * core_ref[0]
    grad[...] = own_ref[...]
    for b in range(2):
        for f in range(4):
            grad[b, f, near_row] += given_ref[50 + b * 6 + f].astype(F32)
            grad[b, f, 3 - near_row] += far_ref[b, 2 + f].astype(F32)
            for h in range(4):
                x = grad[b, f, h]
                if f >= 2:
                    x = x + next_ref[b, f - 2, h].astype(F32)
                x = x.astype(BF)
                top = (b * 2 + h % 2) * 16
                col = (f * 2 + h // 2) * 128
                rows[top : top + 16, col : col + 128] = x
                rows[64 + top : 80 + top, col : col + 128] = pltpu.roll(x.astype(F32), 127, 1).astype(BF)
    place = send_ref[...]
    lane = lax.broadcasted_iota(jnp.int32, (512, 128), 1)
    send = jnp.concatenate([ones_where(place == lane + i * 128) for i in range(8)], axis=1)
    tokens = matmul_nt(send, rows[...]).reshape(64, 2, 4, 128)
    out_ref[:, 0:2] = tokens.astype(BF)
    part = (part_ref[...] + twin_ref[...]) * (0.5 / math.sqrt(4 * 16 * 128 * 128))
    for i in range(3):
        piece = part[:, i * 128 : i * 128 + 128].astype(BF)
        out_ref[:, 2 + i] = jnp.broadcast_to(piece[None], (64, 4, 128))


def take_body(core_ref, mine_ref, other_ref, take_ref, out_ref, wg_ref):
    core = core_ref[0]
    got = jnp.concatenate([ref[:, core].astype(F32).reshape(256, 128) for ref in (mine_ref, other_ref)]).astype(BF)
    src = lax.broadcasted_iota(jnp.int32, (128, 128), 0)
    dst = lax.broadcasted_iota(jnp.int32, (128, 128), 1)
    lane = lax.broadcasted_iota(jnp.int32, (256, 128), 1)
    want = ((dst & 1) << 6) + (((dst >> 1) & 1) << 4) + ((dst >> 2) & 15)
    takes = []
    for e in range(2):
        row = take_ref[e]
        takes.append(jnp.concatenate([ones_where(row == lane + i * 128) for i in range(4)], axis=1))
    for b in range(2):
        total = None
        for e in range(2):
            place = ones_where((src == want + b * 32) & ((dst >> 6) == e))
            moved = matmul(got, place).astype(BF)
            term = matmul(takes[e], moved)
            total = term if total is None else total + term
        out_ref[b] = total.astype(BF)
    for i in range(3):
        mine = mine_ref[:, 2 + i].astype(F32)
        other = other_ref[:, 2 + i].astype(F32)
        cols = slice(i * 128, i * 128 + 128)
        wg_ref[0:256, cols] = jnp.where(core == 0, mine, other).reshape(256, 128)
        wg_ref[256:432, cols] = jnp.where(core == 0, other, mine)[0:44].reshape(176, 128)


def shifted(value, step):
    count = lax.axis_size("tm")
    return lax.ppermute(value, "tm", [(i, i + step) for i in range(count) if 0 <= i + step < count])


def crossed(value):
    count = math.prod(lax.axis_size(a) for a in BAND)
    pairs = [(i, i + 1) for i in range(1, count - 1, 2)]
    return lax.ppermute(value, BAND, pairs + [(j, i) for i, j in pairs])


def swapped(value):
    return lax.ppermute(value, "core", [(0, 1), (1, 0)])


def exchange(value, axes):
    return lax.all_to_all(value, axes, split_axis=0, concat_axis=0, tiled=True)


def whole(shape):
    return pl.BlockSpec(shape, lambda b, f: (0,) * len(shape))


def on_device(latent, weight, cotangent, groups, order):
    tm = lax.axis_index("tm")
    core = lax.axis_index("core")
    me = tm * 32 + lax.axis_index(BAND)
    smem = pl.BlockSpec(memory_space=pltpu.SMEM)
    vmem = pl.BlockSpec(memory_space=pltpu.VMEM)
    hbm = pl.BlockSpec(memory_space=pltpu.HBM)
    lat = latent.transpose(3, 0, 2, 1, 4)
    prev = shifted(lat[:, :, 2:4], 1)
    wide, tall, masks = call(
        weight_body,
        (
            jax.ShapeDtypeStruct((384, 512), BF),
            jax.ShapeDtypeStruct((432, 384), BF),
            jax.ShapeDtypeStruct((24,), jnp.int32),
        ),
        (1e6, 2e6),
        scratch=[pltpu.VMEM((512, 384), F32)],
        in_specs=[smem, smem, vmem],
        out_specs=[vmem] * 2 + [smem],
        vmem=52,
    )(me.reshape(1), groups, weight.T)
    prev, masks = lax.optimization_barrier((prev, masks))
    edge = lambda row: jnp.concatenate([lax.dynamic_index_in_dim(x, row, 0, False) for x in (prev, lat)], axis=1)
    far = crossed(edge(3 * core))
    near = swapped(edge(3 - 3 * core))
    send, take = call(
        select_body,
        (jax.ShapeDtypeStruct((512, 128), jnp.int32), jax.ShapeDtypeStruct((2, 256, 128), jnp.int32)),
        (500e6, 2e6),
        in_specs=[smem, vmem],
        out_specs=[vmem] * 2,
        vmem=52,
    )(me.reshape(1), order.reshape(512, 128))
    far, send = lax.optimization_barrier((far, send))
    keep, pair, grad, gfar, gprev = call(
        main_body,
        tuple(jax.ShapeDtypeStruct(*out) for out in MAIN_OUTS),
        (4.5e9, 5e6),
        scratch=[pltpu.VMEM(*x) for x in MAIN_SCRATCH] + [pltpu.SemaphoreType.DMA((8,))],
        in_specs=[smem, smem] + [vmem] * 4 + [hbm] + [vmem] * 2,
        out_specs=[vmem] * 5,
        vmem=52,
    )(core.reshape(1), masks, prev, lat, near, far, cotangent, wide, tall)
    from_far = crossed(gfar)
    given = swapped(pair)
    half = call(add_body, jax.ShapeDtypeStruct((64, 4, 384), BF), (1e5, 3e7), in_specs=[vmem] * 2)(keep, given)
    early = call(
        early_body,
        jax.ShapeDtypeStruct((2, 2, 4, 16, 128), BF),
        (1e5, 3e5),
        in_specs=[smem] + [vmem] * 3,
    )(core.reshape(1), gprev, given, from_far)
    from_next = shifted(early, -1)
    parts = exchange(half, CHIPS)
    part = jnp.sum(parts.astype(F32), axis=0)
    twin = lax.ppermute(part, "rep", [(0, 1), (1, 0)])
    outgoing = call(
        out_body,
        jax.ShapeDtypeStruct((64, 5, 4, 128), BF),
        (150e6, 2e6),
        scratch=[pltpu.VMEM((128, 1024), BF), pltpu.VMEM((2, 4, 4, 16, 128), F32)],
        in_specs=[smem] + [vmem] * 7,
    )(core.reshape(1), grad, given, from_far, from_next, send, part, twin)
    got = exchange(outgoing, CHIPS)
    other = swapped(got)
    tokens, summed = call(
        take_body,
        (jax.ShapeDtypeStruct((2, 256, 128), BF), jax.ShapeDtypeStruct((432, 384), F32)),
        (200e6, 1e6),
        in_specs=[smem] + [vmem] * 3,
    )(core.reshape(1), got, other, take)
    return tokens, summed.T


def solution(mesh):
    split = Mesh(mesh.devices.reshape(4, 2, 8, 2, 2), ("tm", "xl", "z", "core", "rep"))
    placed = P("rep", None, "tm", BAND, None)
    return jax.shard_map(
        on_device,
        mesh=split,
        in_specs=(placed, P(), placed, P("rep", None), P()),
        out_specs=(P("rep", PEERS, None), P()),
        check_vma=False,
    )
```

```python
import math

import jax
import jax.numpy as jnp
from jax import lax
from jax.experimental import pallas as pl
from jax.experimental.pallas import tpu as pltpu
from jax.sharding import Mesh, PartitionSpec as P

BF = jnp.bfloat16
F32 = jnp.float32
BAND = ("xl", "z", "core")
PEERS = ("tm", "xl", "z", "core")
CHIPS = ("tm", "xl", "z")
NT = (((1,), (1,)), ((), ()))


def matmul(a, b):
    return jnp.dot(a, b, preferred_element_type=F32)


def matmul_nt(a, b):
    return lax.dot_general(a, b, NT, preferred_element_type=F32)


MAIN_OUTS = [
    ((48, 16, 128), BF),
    ((60, 16, 128), BF),
    ((2, 4, 4, 16, 128), F32),
    ((2, 6, 16, 128), BF),
    ((2, 2, 4, 16, 128), F32),
]
MAIN_SCRATCH = [
    ((8, 384, 4, 128), BF),
    ((2, 3, 6, 6, 16, 128), BF),
    ((512, 512), BF),
    ((384, 512), F32),
    ((384, 512), F32),
    ((2, 3, 6, 6, 16, 128), F32),
    ((6, 16, 128), F32),
    ((1544, 128), F32),
    ((384, 512), BF),
    ((512, 384), F32),
    ((512, 512), BF),
    ((384, 512), F32),
]


def call(body, outs, cost, scratch=(), grid=None, in_specs=None, out_specs=None, vmem=16):
    params = {}
    if grid is not None:
        params = {"grid": grid, "in_specs": in_specs, "out_specs": out_specs}
    elif in_specs is not None:
        params = {"in_specs": in_specs}
        if out_specs is not None:
            params["out_specs"] = out_specs
    return pl.pallas_call(
        body,
        out_shape=outs,
        scratch_shapes=list(scratch),
        cost_estimate=pl.CostEstimate(flops=int(cost[0]), bytes_accessed=int(cost[1]), transcendentals=0),
        compiler_params=pltpu.CompilerParams(vmem_limit_bytes=vmem * 1024 * 1024),
        **params,
    )


def ones_where(cond):
    return jnp.where(cond, 1.0, 0.0).astype(BF)


def weight_body(me_ref, seg_ref, wt_ref, wide_ref, copy_ref, mask_ref, tall):
    me = me_ref[0]
    for b in range(2):
        for f in range(4):
            frame = (me >> 5) * 4 + f
            for a in range(3):
                before = frame - (2 - a)
                same = (before >= 0) & (seg_ref[b, jnp.maximum(before, 0)] == seg_ref[b, frame])
                mask_ref[12 * b + 3 * f + a] = jnp.where(same, 1, 0)
    copy_ref[...] = wt_ref[...]
    tall[0:432, :] = wt_ref[...].astype(F32)
    tall[432:512, :] = jnp.zeros((80, 384), F32)
    wide_ref[...] = (tall[...] * 0.5).T.astype(BF)


def select_body(me_ref, order_ref, send_ref, take_ref):
    me = me_ref[0]
    order = order_ref[...]
    mine = ((order >> 14) * 32 + ((order >> 7) & 31)) == me
    local_id = (((order >> 12) & 3) * 2 + ((order >> 6) & 1)) * 64 + (order & 63)
    hits = ones_where(mine)
    up = lax.broadcasted_iota(jnp.int32, (128, 128), 0)
    lane = lax.broadcasted_iota(jnp.int32, (128, 128), 1)
    running = matmul(hits, ones_where(up <= lane))
    row = lax.broadcasted_iota(jnp.int32, (512, 512), 0)
    col = lax.broadcasted_iota(jnp.int32, (512, 512), 1)
    group = (row >> 2) == (col >> 2)
    above = matmul(ones_where(group & (col < row)), hits)
    running = running + jnp.sum(above, axis=1, keepdims=True)
    lane = lax.broadcasted_iota(jnp.int32, (512, 128), 1)
    slot = lax.broadcasted_iota(jnp.int32, (512, 128), 0) & 3
    found = jnp.zeros((512, 128), F32)
    for s in range(4):
        hit = mine & (running == s + 1.0)
        high = jnp.sum(jnp.where(hit, local_id >> 4, 0).astype(F32), axis=1, keepdims=True)
        low = jnp.sum(jnp.where(hit, local_id & 15, 0).astype(F32), axis=1, keepdims=True)
        found = found + jnp.where(lane == s, high, 0.0) + jnp.where(lane == s + 4, low, 0.0)
    found = matmul(ones_where(group), found.astype(BF))
    found = jnp.where(lane == slot, found * 16.0, 0.0) + jnp.where(lane == slot + 4, found, 0.0)
    place = 2 * jnp.sum(found, axis=1, keepdims=True).astype(jnp.int32)
    send_ref[...] = jnp.broadcast_to(place, (512, 128))
    pair = order_ref[pl.ds(pl.multiple_of((me >> 1) * 8, 8), 8), :]
    four = jnp.where((me & 1) == 0, pair[0:4], pair[4:8])
    own = jnp.concatenate([four[i : i + 1] for i in range(4)], axis=1)
    sender = (own >> 14) * 32 + ((own >> 7) & 31)
    pos = lax.broadcasted_iota(jnp.int32, (256, 512), 1)
    half = lax.broadcasted_iota(jnp.int32, (256, 512), 0)
    for e in range(2):
        here = pos == 2 * half + e
        mate = jnp.sum(jnp.where(here, sender, 0).astype(F32), axis=1, keepdims=True).astype(jnp.int32)
        earlier = (sender == mate) & (pos < 2 * half + e)
        count = jnp.sum(jnp.where(earlier, 1.0, 0.0), axis=1, keepdims=True)
        far = jnp.where((mate & 1) == (me & 1), 0, 256)
        take_ref[e] = jnp.broadcast_to(far + (mate >> 1) * 4 + count.astype(jnp.int32), (256, 128))


def main_body(
    core_ref, mask_ref, prev, lat, near, far, cot_hbm, wide, wt, keep, pair, own, gfar, gprev,
    cot, ext, patch, pre, total, spread, edges, cots, grad, turned, patch1, pre1, cot_sems,
):
    lanes = lax.broadcasted_iota(jnp.int32, (1, 128), 1)
    near_row = 5 - 5 * core_ref[0]

    def cot_copy(i):
        return pltpu.make_async_copy(cot_hbm.at[i >> 2, :, i & 3], cot.at[i], cot_sems.at[i])

    for i in range(8):
        cot_copy(i).start()
    patch[432:512, :] = jnp.zeros((80, 512), BF)
    patch1[432:512, :] = jnp.zeros((80, 512), BF)
    total[...] = jnp.zeros_like(total)
    spread[...] = jnp.zeros_like(spread)
    for b in range(2):
        for h in range(4):
            ext[b, 1, 0:2, 1 + h] = prev[h, b]
            ext[b, 1, 2:6, 1 + h] = lat[h, b]
        ext[b, 1, :, near_row] = near[b]
        ext[b, 1, :, 5 - near_row] = far[b]
        for fr in range(6):
            x = ext[b, 1, fr].astype(F32).reshape(96, 128)
            left = jnp.where(lanes == 0, 0.0, pltpu.roll(x, 1, 1))
            right = jnp.where(lanes == 127, 0.0, pltpu.roll(x, 127, 1))
            ext[b, 0, fr] = left.astype(BF).reshape(6, 16, 128)
            ext[b, 2, fr] = right.astype(BF).reshape(6, 16, 128)

    def factors(i):
        return [mask_ref[3 * i + a].astype(F32) for a in range(3)]

    def build(i, patch):
        b, f = i >> 2, i & 3
        masks = factors(i)
        for a in range(3):
            mask = jnp.full((16, 128), masks[a], F32).astype(BF)
            for r in range(3):
                for c in range(3):
                    top = (a * 9 + r * 3 + c) * 16
                    for h in range(4):
                        patch[top : top + 16, h * 128 : h * 128 + 128] = ext[b, c, f + a, h + r] * mask

    def relayout(i):
        cot_copy(i).wait()
        cots[0:1536] = cot[i].astype(F32).reshape(1536, 128)

    def elements(h, pre):
        x = pre[:, h * 128 : h * 128 + 128]
        t = jnp.tanh(x)
        cot = cots[pl.ds(h, 384, stride=4), :]
        grad[:, h * 128 : h * 128 + 128] = (cot * (1.0 + t) * (1.0 + x * (1.0 - t))).astype(BF)

    def spread_tap(i, a, back):
        b, f = i >> 2, i & 3
        mask = factors(i)[a]
        for c in range(3):
            for row in range(6):
                acc = None
                for r in range(3):
                    h = row - r
                    if 0 <= h < 4:
                        top = (r * 3 + c) * 16
                        term = back[top : top + 16, h * 128 : h * 128 + 128]
                        acc = term if acc is None else acc + term
                spread[b, c, f + a, row] += acc * mask

    def advance(i, patch, pre, next_patch, next_pre):
        build(jnp.minimum(i + 1, 7), next_patch)
        relayout(i)
        next_pre[...] = matmul(wide[...], next_patch[...])
        for h in range(4):
            elements(h, pre)
        back = matmul(wt[...], grad[...])
        total[...] += matmul_nt(grad[...], patch[...])
        for a in range(3):
            spread_tap(i, a, back[a * 144 : a * 144 + 144])

    build(0, patch)
    pre[...] = matmul(wide[...], patch[...])

    def step(j, carry):
        advance(2 * j, patch, pre, patch1, pre1)
        advance(2 * j + 1, patch1, pre1, patch, pre)
        return carry

    lax.fori_loop(0, 4, step, 0)
    turned[...] = total[...].T
    mine = core_ref[0] * 256
    for g in range(16):
        for i in range(3):
            cols = slice(i * 128, i * 128 + 128)
            kept = pl.multiple_of(mine + g * 16, 16)
            pair[g * 3 + i] = turned[pl.ds(pl.multiple_of(256 - mine + g * 16, 16), 16), cols].astype(BF)
            keep[g * 3 + i] = turned[pl.ds(kept, 16), cols].astype(BF)
    for b in range(2):
        for fr in range(6):
            x0 = spread[b, 0, fr].reshape(96, 128)
            x2 = spread[b, 2, fr].reshape(96, 128)
            x = (
                spread[b, 1, fr].reshape(96, 128)
                + jnp.where(lanes == 127, 0.0, pltpu.roll(x0, 127, 1))
                + jnp.where(lanes == 0, 0.0, pltpu.roll(x2, 1, 1))
            ).reshape(6, 16, 128) * 0.5
            edges[0] = x[0]
            edges[5] = x[5]
            pair[48 + b * 6 + fr] = edges[near_row].astype(BF)
            gfar[b, fr] = edges[5 - near_row].astype(BF)
            if fr < 2:
                gprev[b, fr] = x[1:5]
            else:
                own[b, fr - 2] = x[1:5]


def add_body(keep_ref, given_ref, out_ref):
    for g in range(16):
        for i in range(3):
            x = keep_ref[g * 3 + i].astype(F32) + given_ref[g * 3 + i].astype(F32)
            out_ref[g * 4 : g * 4 + 4, :, i * 128 : i * 128 + 128] = x.reshape(4, 4, 128).astype(BF)


def early_body(core_ref, gprev_ref, given_ref, far_ref, out_ref):
    near_row = 3 - 3 * core_ref[0]
    out_ref[...] = gprev_ref[...].astype(BF)
    for b in range(2):
        for f in range(2):
            near = given_ref[48 + b * 6 + f].astype(F32)
            out_ref[b, f, near_row] = (gprev_ref[b, f, near_row] + near).astype(BF)
            far = far_ref[b, f].astype(F32)
            out_ref[b, f, 3 - near_row] = (gprev_ref[b, f, 3 - near_row] + far).astype(BF)


def out_body(core_ref, own_ref, given_ref, far_ref, next_ref, send_ref, part_ref, twin_ref, out_ref, rows, grad):
    near_row = 3 - 3 * core_ref[0]
    grad[...] = own_ref[...]
    for b in range(2):
        for f in range(4):
            grad[b, f, near_row] += given_ref[50 + b * 6 + f].astype(F32)
            grad[b, f, 3 - near_row] += far_ref[b, 2 + f].astype(F32)
            for h in range(4):
                x = grad[b, f, h]
                if f >= 2:
                    x = x + next_ref[b, f - 2, h].astype(F32)
                x = x.astype(BF)
                top = (b * 2 + h % 2) * 16
                col = (f * 2 + h // 2) * 128
                rows[top : top + 16, col : col + 128] = x
                rows[64 + top : 80 + top, col : col + 128] = pltpu.roll(x.astype(F32), 127, 1).astype(BF)
    place = send_ref[...]
    lane = lax.broadcasted_iota(jnp.int32, (512, 128), 1)
    send = jnp.concatenate([ones_where(place == lane + i * 128) for i in range(8)], axis=1)
    tokens = matmul_nt(send, rows[...]).reshape(64, 2, 4, 128)
    out_ref[:, 0:2] = tokens.astype(BF)
    part = (part_ref[...] + twin_ref[...]) * (0.5 / math.sqrt(4 * 16 * 128 * 128))
    for i in range(3):
        piece = part[:, i * 128 : i * 128 + 128].astype(BF)
        out_ref[:, 2 + i] = jnp.broadcast_to(piece[None], (64, 4, 128))


def taken(core, rows_ref, take_ref, first):
    got = rows_ref[:, core].astype(F32).reshape(256, 128).astype(BF)
    src = lax.broadcasted_iota(jnp.int32, (128, 128), 0)
    dst = lax.broadcasted_iota(jnp.int32, (128, 128), 1)
    lane = lax.broadcasted_iota(jnp.int32, (256, 128), 1)
    want = ((dst & 1) << 6) + (((dst >> 1) & 1) << 4) + ((dst >> 2) & 15)
    takes = []
    for e in range(2):
        row = take_ref[e] - first
        takes.append(jnp.concatenate([ones_where(row == lane + i * 128) for i in range(2)], axis=1))
    result = []
    for b in range(2):
        total = None
        for e in range(2):
            place = ones_where((src == want + b * 32) & ((dst >> 6) == e))
            term = matmul(takes[e], matmul(got, place).astype(BF))
            total = term if total is None else total + term
        result.append(total)
    return result


def own_body(core_ref, mine_ref, take_ref, part_ref):
    for b, x in enumerate(taken(core_ref[0], mine_ref, take_ref, 0)):
        part_ref[b] = x.astype(BF)


def take_body(core_ref, mine_ref, other_ref, take_ref, part_ref, out_ref, wg_ref):
    core = core_ref[0]
    for b, x in enumerate(taken(core, other_ref, take_ref, 256)):
        out_ref[b] = (part_ref[b].astype(F32) + x).astype(BF)
    for i in range(3):
        mine = mine_ref[:, 2 + i].astype(F32)
        other = other_ref[:, 2 + i].astype(F32)
        cols = slice(i * 128, i * 128 + 128)
        wg_ref[0:256, cols] = jnp.where(core == 0, mine, other).reshape(256, 128)
        wg_ref[256:432, cols] = jnp.where(core == 0, other, mine)[0:44].reshape(176, 128)


def shifted(value, step):
    count = lax.axis_size("tm")
    return lax.ppermute(value, "tm", [(i, i + step) for i in range(count) if 0 <= i + step < count])


def crossed(value):
    count = math.prod(lax.axis_size(a) for a in BAND)
    pairs = [(i, i + 1) for i in range(1, count - 1, 2)]
    return lax.ppermute(value, BAND, pairs + [(j, i) for i, j in pairs])


def swapped(value):
    return lax.ppermute(value, "core", [(0, 1), (1, 0)])


def exchange(value, axes):
    return lax.all_to_all(value, axes, split_axis=0, concat_axis=0, tiled=True)


def whole(shape):
    return pl.BlockSpec(shape, lambda b, f: (0,) * len(shape))


def on_device(latent, weight, cotangent, groups, order):
    tm = lax.axis_index("tm")
    core = lax.axis_index("core")
    me = tm * 32 + lax.axis_index(BAND)
    smem = pl.BlockSpec(memory_space=pltpu.SMEM)
    vmem = pl.BlockSpec(memory_space=pltpu.VMEM)
    hbm = pl.BlockSpec(memory_space=pltpu.HBM)
    lat = latent.transpose(3, 0, 2, 1, 4)
    prev = shifted(lat[:, :, 2:4], 1)
    wide, tall, masks = call(
        weight_body,
        (
            jax.ShapeDtypeStruct((384, 512), BF),
            jax.ShapeDtypeStruct((432, 384), BF),
            jax.ShapeDtypeStruct((24,), jnp.int32),
        ),
        (1e6, 2e6),
        scratch=[pltpu.VMEM((512, 384), F32)],
        in_specs=[smem, smem, vmem],
        out_specs=[vmem] * 2 + [smem],
        vmem=52,
    )(me.reshape(1), groups, weight.T)
    prev, masks = lax.optimization_barrier((prev, masks))
    edge = lambda row: jnp.concatenate([lax.dynamic_index_in_dim(x, row, 0, False) for x in (prev, lat)], axis=1)
    far = crossed(edge(3 * core))
    near = swapped(edge(3 - 3 * core))
    send, take = call(
        select_body,
        (jax.ShapeDtypeStruct((512, 128), jnp.int32), jax.ShapeDtypeStruct((2, 256, 128), jnp.int32)),
        (500e6, 2e6),
        in_specs=[smem, vmem],
        out_specs=[vmem] * 2,
        vmem=52,
    )(me.reshape(1), order.reshape(512, 128))
    far, send = lax.optimization_barrier((far, send))
    keep, pair, grad, gfar, gprev = call(
        main_body,
        tuple(jax.ShapeDtypeStruct(*out) for out in MAIN_OUTS),
        (4.5e9, 5e6),
        scratch=[pltpu.VMEM(*x) for x in MAIN_SCRATCH] + [pltpu.SemaphoreType.DMA((8,))],
        in_specs=[smem, smem] + [vmem] * 4 + [hbm] + [vmem] * 2,
        out_specs=[vmem] * 5,
        vmem=52,
    )(core.reshape(1), masks, prev, lat, near, far, cotangent, wide, tall)
    from_far = crossed(gfar)
    given = swapped(pair)
    half = call(add_body, jax.ShapeDtypeStruct((64, 4, 384), BF), (1e5, 3e7), in_specs=[vmem] * 2)(keep, given)
    early = call(
        early_body,
        jax.ShapeDtypeStruct((2, 2, 4, 16, 128), BF),
        (1e5, 3e5),
        in_specs=[smem] + [vmem] * 3,
    )(core.reshape(1), gprev, given, from_far)
    from_next = shifted(early, -1)
    parts = exchange(half, CHIPS)
    part = jnp.sum(parts.astype(F32), axis=0)
    twin = lax.ppermute(part, "rep", [(0, 1), (1, 0)])
    outgoing = call(
        out_body,
        jax.ShapeDtypeStruct((64, 5, 4, 128), BF),
        (150e6, 2e6),
        scratch=[pltpu.VMEM((128, 1024), BF), pltpu.VMEM((2, 4, 4, 16, 128), F32)],
        in_specs=[smem] + [vmem] * 7,
    )(core.reshape(1), grad, given, from_far, from_next, send, part, twin)
    got = exchange(outgoing, CHIPS)
    other = swapped(got)
    part = call(
        own_body,
        jax.ShapeDtypeStruct((2, 256, 128), BF),
        (100e6, 1e6),
        in_specs=[smem] + [vmem] * 2,
    )(core.reshape(1), got, take)
    tokens, summed = call(
        take_body,
        (jax.ShapeDtypeStruct((2, 256, 128), BF), jax.ShapeDtypeStruct((432, 384), F32)),
        (200e6, 1e6),
        in_specs=[smem] + [vmem] * 4,
    )(core.reshape(1), got, other, take, part)
    return tokens, summed.T


def solution(mesh):
    split = Mesh(mesh.devices.reshape(4, 2, 8, 2, 2), ("tm", "xl", "z", "core", "rep"))
    placed = P("rep", None, "tm", BAND, None)
    return jax.shard_map(
        on_device,
        mesh=split,
        in_specs=(placed, P(), placed, P("rep", None), P()),
        out_specs=(P("rep", PEERS, None), P()),
        check_vma=False,
    )
```
